32 devices in a mesh: section: 2 (over y), seq: 16 (over z, x, core).
Axes of the slice: x: 2, y: 2, z: 4, core: 2. Of those that a mesh axis runs over, the one named last changes fastest.
Arguments:
- activations: bfloat16 [2, 2048, 3584], P('section', 'seq'), may hold values from -80 to 80
- incoming: bfloat16 [2048, 3584], P('seq'), may hold values from -4 to 4
- column_ids: int32 [3, 2048], replicated, may hold values from 0 to 11, as said below
- positions: int32 [3, 2048], replicated, may hold values from 0 to 23, as said below
- norm_gain: float32 [2, 3584], P('section')
- w_query: bfloat16 [2, 3584, 1792], P('section', 'seq')
- w_key: bfloat16 [2, 3584, 256], P('section', 'seq')
- w_value: bfloat16 [2, 3584, 256], P('section', 'seq'), may hold values from -0.09375 to 0.09375
- w_out: bfloat16 [2, 1792, 3584], P('section', 'seq'), may hold values from -0.125 to 0.125
- b_query: float32 [2, 1792], P('section'), may hold values from -4 to 4
- b_key: float32 [2, 256], P('section'), may hold values from -4 to 4
- b_value: float32 [2, 256], P('section'), may hold values from -3 to 3
Outputs:
- first_pass: bfloat16 [2, 2048, 3584], P('section', 'seq')
- second_pass: bfloat16 [2, 2048, 3584], P('section', 'seq')
The draws below stay inside these ranges and needn't reach their ends.
Inputs may be any that keep to these rules, and one draw needn't show every extreme that they name: `column_ids`: each row is one serialized table: runs of one or two consecutive tokens form cells, the cells take the column numbers 0, 1, ..., 11 in turn, table row after table row; column 0 is a row's header cell. The first table row of every micro-batch has two tokens in each cell. `positions`: A token's position counts the tokens since its table row began.
All inputs are finite; a program needn't handle non-finite values.
Results may differ from the reference program's by a relative error of at most 0.012.
Values may be sent and summed in bfloat16 or wider, within the bound.
A program may use at most 128 MiB of HBM per device.

```python
import math
import jax
import jax.numpy as jnp
from jax import lax

D = 3584
HEAD_DIM = 128
HEADS = 14
KV_HEADS = 2
NCOL = 12
QW = 1792
KVW = 256
SEQ = 2048
SECTIONS = 2
MICRO = 3
N_SECTION = 2


def table_layout(key):
    index = jnp.broadcast_to(jnp.arange(SEQ, dtype=jnp.int32)[None, :], (MICRO, SEQ))
    random_starts = jax.random.randint(key, (MICRO, SEQ), 0, 2) == 0
    random_starts = random_starts | (index == 2 * NCOL)
    previous = jnp.concatenate([jnp.ones((MICRO, 1), jnp.bool_), random_starts[:, :-1]], axis=1)
    random_starts = random_starts | jnp.logical_not(previous)
    leading = index < 2 * NCOL
    starts = jnp.where(leading, index % 2 == 0, random_starts)
    starts = starts | (index == 0) | (index == 2 * NCOL)
    cells = jnp.cumsum(starts.astype(jnp.int32), axis=1) - 1
    columns = cells % NCOL
    row_start = starts & (columns == 0)
    begins = lax.cummax(jnp.where(row_start, index, 0), axis=1)
    return (columns.astype(jnp.int32), (index - begins).astype(jnp.int32))


def draw_column_ids(key, part):
    columns, places = table_layout(jax.random.fold_in(key, 31))
    return columns


def draw_positions(key, part):
    columns, places = table_layout(jax.random.fold_in(key, 31))
    return places


def draw_activations(key, part):
    shape = (SECTIONS, SEQ, D)
    base = jax.random.truncated_normal(jax.random.fold_in(key, 3), -4.0, 4.0, shape, jnp.float32)
    return base.astype(jnp.bfloat16)


def draw_norm_gain(key, part):
    shape = (SECTIONS, D)
    return jnp.exp(jax.random.uniform(key, shape, jnp.float32, math.log(0.5), math.log(2.0)))


def query_base(key):
    return jax.random.truncated_normal(jax.random.fold_in(key, 101), -4.0, 4.0, (SECTIONS, D, HEADS * HEAD_DIM), jnp.float32) * D ** (-0.5)


def draw_w_query(key, part):
    return query_base(key).astype(jnp.bfloat16)


def draw_w_key(key, part):
    noise = jax.random.truncated_normal(jax.random.fold_in(key, 202), -4.0, 4.0, (SECTIONS, D, KV_HEADS * HEAD_DIM), jnp.float32) * D ** (-0.5)
    return noise.astype(jnp.bfloat16)


def block_scale(stream_key, shape, pieces, least, top_value):
    def one(axis_at, blocks):
        steps = jax.random.uniform(jax.random.fold_in(jax.random.fold_in(stream_key, 6), axis_at), (blocks,), jnp.float32, least / len(pieces), top_value / len(pieces))
        return jnp.repeat(jnp.exp(steps), shape[axis_at] // blocks).reshape((-1,) + (1,) * (len(shape) - axis_at - 1))

    level = one(*pieces[0])
    for cut in pieces[1:]:
        level = level * one(*cut)
    return level


def centred(key, shape, scale, reach, shards=(), kind=jnp.bfloat16):
    values = jax.random.normal(key, shape, jnp.float32) * scale
    if len(shards) > 0:
        values = block_scale(key, shape, shards, -0.22, 0.18) * values
    return jnp.clip(values, min=-reach, max=reach).astype(kind)


def setup_inputs(seed: int = 0) -> dict:
    key_of = jax.random.split(jax.random.key(seed), 13)
    return {
        "activations": draw_activations(jax.random.fold_in(key_of[12], 71), 0),
        "incoming": centred(key_of[1], (SEQ, D), 1.0, 4.0, ((0, 16),)),
        "column_ids": draw_column_ids(jax.random.fold_in(key_of[12], 71), 0),
        "positions": draw_positions(jax.random.fold_in(key_of[12], 71), 0),
        "norm_gain": draw_norm_gain(jax.random.fold_in(key_of[12], 71), 0),
        "w_query": draw_w_query(jax.random.fold_in(key_of[12], 71), 0),
        "w_key": draw_w_key(jax.random.fold_in(key_of[12], 71), 0),
        "w_value": centred(key_of[7], (SECTIONS, D, KVW), D ** -0.5, 0.09375, ((0, 2), (1, 16))),
        "w_out": centred(key_of[8], (SECTIONS, QW, D), QW ** -0.5, 0.125, ((0, 2), (1, 16))),
        "b_query": centred(key_of[9], (SECTIONS, QW), 1.0, 4.0, ((0, 2),), jnp.float32),
        "b_key": centred(key_of[10], (SECTIONS, KVW), 1.0, 4.0, ((0, 2),), jnp.float32),
        "b_value": centred(key_of[11], (SECTIONS, KVW), 0.5, 3.0, ((0, 2),), jnp.float32),
    }


EPSILON = 1e-06
THETA = 1000000.0

def rotate(entries, places):
    half = entries.shape[-1] // 2
    freqs = THETA ** (-(jnp.arange(half, dtype=jnp.float32) * 2.0) / entries.shape[-1])
    angles = places.astype(jnp.float32)[:, None] * freqs[None, :]
    cosine = jnp.cos(angles)[:, None, :]
    sine = jnp.sin(angles)[:, None, :]
    first = entries[..., :half]
    second = entries[..., half:]
    return jnp.concatenate([first * cosine - second * sine, second * cosine + first * sine], axis=-1)

def section_layer(inputs, gain, query_weight, key_weight, value_weight, out_weight, query_bias, key_bias, value_bias, columns, places):
    length = inputs.shape[0]
    wide = inputs.astype(jnp.float32)
    hidden = (wide * lax.rsqrt(lax.optimization_barrier(jnp.mean(wide * wide, axis=-1, keepdims=True)) + EPSILON) * gain).astype(jnp.bfloat16)
    queries = rotate((jnp.dot(hidden, query_weight, preferred_element_type=jnp.float32) + query_bias).reshape(length, HEADS, HEAD_DIM), places).astype(jnp.bfloat16)
    keys_rot = rotate((jnp.dot(hidden, key_weight, preferred_element_type=jnp.float32) + key_bias).reshape(length, KV_HEADS, HEAD_DIM), places).astype(jnp.bfloat16)
    values = (jnp.dot(hidden, value_weight, preferred_element_type=jnp.float32) + value_bias).astype(jnp.bfloat16).reshape(length, KV_HEADS, HEAD_DIM)
    index = jnp.arange(length, dtype=jnp.int32)
    allowed = (index[None, :] <= index[:, None]) & ((columns[None, :] == columns[:, None]) | (columns[None, :] == 0))
    group = HEADS // KV_HEADS
    scale = HEAD_DIM ** (-0.5)
    head_queries = jnp.transpose(queries, (1, 0, 2))
    head_keys = jnp.repeat(jnp.transpose(keys_rot, (1, 0, 2)), group, axis=0)
    head_values = jnp.repeat(jnp.transpose(values, (1, 0, 2)), group, axis=0)

    def one_head(operands):
        query_head, key_head, value_head = operands
        scores = jnp.dot(query_head, key_head.T, preferred_element_type=jnp.float32) * scale
        scores = jnp.where(allowed, scores, -1e+30)
        top = lax.optimization_barrier(jnp.max(scores, axis=-1, keepdims=True))
        exponentials = jnp.where(allowed, jnp.exp(scores - top), 0.0)
        probs = exponentials.astype(jnp.bfloat16)
        summed = jnp.dot(probs, value_head, preferred_element_type=jnp.float32)
        return summed / lax.optimization_barrier(jnp.sum(exponentials, axis=-1, keepdims=True))
    mixed = lax.map(one_head, (head_queries, head_keys, head_values))
    context = jnp.transpose(mixed, (1, 0, 2)).reshape(length, HEADS * HEAD_DIM).astype(jnp.bfloat16)
    return (wide + jnp.dot(context, out_weight, preferred_element_type=jnp.float32)).astype(jnp.bfloat16)

def apply_section(inputs, layer_index, micro_row, norm_gain, w_query, w_key, w_value, w_out, b_query, b_key, b_value, column_ids, positions):
    return section_layer(inputs, norm_gain[layer_index], w_query[layer_index], w_key[layer_index], w_value[layer_index], w_out[layer_index], b_query[layer_index], b_key[layer_index], b_value[layer_index], column_ids[micro_row], positions[micro_row])

def reference(activations, incoming, column_ids, positions, norm_gain, w_query, w_key, w_value, w_out, b_query, b_key, b_value):
    firsts = []
    for layer_index in range(N_SECTION):
        firsts.append(apply_section(activations[layer_index], layer_index, layer_index, norm_gain, w_query, w_key, w_value, w_out, b_query, b_key, b_value, column_ids, positions))
    seconds = []
    for layer_index in range(N_SECTION):
        if layer_index == 0:
            source = incoming
            micro_row = N_SECTION
        else:
            source = firsts[layer_index - 1]
            micro_row = layer_index - 1
        seconds.append(apply_section(source, layer_index, micro_row, norm_gain, w_query, w_key, w_value, w_out, b_query, b_key, b_value, column_ids, positions))
    return (jnp.stack(firsts), jnp.stack(seconds))
```

```python
import functools
import math

import jax
import jax.numpy as jnp
from jax import lax
from jax.experimental import pallas as pl
from jax.experimental.pallas import tpu as pltpu
from jax.sharding import PartitionSpec as P

HEAD_DIM = 128
HEADS = 14
KV_HEADS = 2
EPSILON = 1e-06
THETA = 1000000.0
MESH = pl.DeviceIdType.MESH

PLANES, CHIPS_X, CORES = 4, 2, 2
CHIPS = PLANES * CHIPS_X


def kernel(
    n_section,
    dims,
    x_ref,
    inc_ref,
    wq_ref,
    wk_ref,
    wv_ref,
    wo_ref,
    gain_ref,
    bias_ref,
    cos_ref,
    sin_ref,
    qcol_ref,
    kcol_ref,
    out1_ref,
    out2_ref,
    wqkv,
    wout,
    xs1,
    xs2,
    hidden,
    acc,
    qs,
    kv1,
    kv2,
    mask,
    ctx1,
    ctx2,
    half1,
    half2,
    loc_sem,
    cx_send,
    cx_recv,
    up_send,
    up_recv,
    dn_send,
    dn_recv,
    xl_send,
    xl_recv,
    kv_send,
    kv_recv,
    ps_send,
    ps_recv,
):
    (rows, d, qw, kvw) = dims
    seq_len = rows * CHIPS * CORES
    tok = rows * CORES
    qh, kh, oh = qw // CORES, kvw // CORES, d // CORES
    group = HEADS // KV_HEADS
    wr, wor = wq_ref.shape[0], wo_ref.shape[0]

    s = lax.axis_index("section")
    me = lax.axis_index("seq")
    chip = me // CORES
    c = me % CORES
    z = chip // CHIPS_X
    x = chip % CHIPS_X
    oc = 1 - c
    ox = 1 - x

    def dev(zz, xx, cc):
        return (s, (zz * CHIPS_X + xx) * CORES + cc)

    partner = dev(z, x, oc)
    x_peer = dev(z, ox, c)
    z_up = dev(jnp.minimum(z + 1, PLANES - 1), x, c)
    z_dn = dev(jnp.maximum(z - 1, 0), x, c)

    sent = []

    def send(src, dst, ssem, rsem, target, cond=None):
        copy = pltpu.make_async_remote_copy(
            src_ref=src, dst_ref=dst, send_sem=ssem, recv_sem=rsem,
            device_id=target, device_id_type=MESH,
        )
        if cond is None:
            copy.start()
        else:
            pl.when(cond)(copy.start)
        sent.append((copy, cond))

    def arrived(ref, rsem, ssem, target):
        pltpu.make_async_remote_copy(
            src_ref=ref, dst_ref=ref, send_sem=ssem, recv_sem=rsem,
            device_id=target, device_id_type=MESH,
        ).wait_recv()

    def at(offset, size, unit=16):
        return pl.ds(pl.multiple_of(offset, unit), size)

    barrier = pltpu.get_barrier_semaphore()

    def greet(target):
        pl.semaphore_signal(barrier, inc=1, device_id=target, device_id_type=MESH)

    greet(partner)
    for step in range(1, CHIPS):
        greet((s, lax.rem(chip + step, CHIPS) * CORES + c))
    has_prev = s > 0
    has_next = s < n_section - 1
    s_prev = (jnp.maximum(s - 1, 0), me)
    s_next = (jnp.minimum(s + 1, n_section - 1), me)
    pl.when(has_prev)(lambda: greet(s_prev))
    pl.when(has_next)(lambda: greet(s_next))
    pl.semaphore_wait(barrier, CHIPS + has_prev.astype(jnp.int32) + has_next.astype(jnp.int32))

    row0 = chip * (CORES * wr) + c * wr
    orow0 = chip * (CORES * wr) + oc * wr
    wrow0 = chip * (CORES * wor) + c * wor
    worow0 = chip * (CORES * wor) + oc * wor
    pieces = [
        (wq_ref, wqkv, row0, orow0, wr, 0, qh),
        (wk_ref, wqkv, row0, orow0, wr, qh, kh),
        (wv_ref, wqkv, row0, orow0, wr, qh + kh, kh),
        (wo_ref, wout, wrow0, worow0, wor, 0, oh),
    ]
    local = []
    for i, (src, dst, r0, _, n, col, width) in enumerate(pieces):
        there = dst.at[at(r0, n), pl.ds(col, width)]
        send(src.at[:, at(oc * width, width, 128)], there, cx_send.at[i], cx_recv.at[i], partner)
        copy = pltpu.make_async_copy(src.at[:, at(c * width, width, 128)], there, loc_sem.at[i])
        copy.start()
        local.append(copy)

    mine = at(c * rows, rows)
    send(x_ref, xs1.at[mine], cx_send.at[4], cx_recv.at[4], partner)
    copy = pltpu.make_async_copy(x_ref, xs1.at[mine], loc_sem.at[4])
    copy.start()
    local.append(copy)
    first = s == 0
    send(inc_ref, xs2.at[mine], cx_send.at[5], cx_recv.at[5], partner, first)
    inc_copy = pltpu.make_async_copy(inc_ref, xs2.at[mine], loc_sem.at[5])
    pl.when(first)(inc_copy.start)

    def own_ready(i):
        _, dst, _, r1, n, col, width = pieces[i]
        local[i].wait()
        arrived(dst.at[at(r1, n), pl.ds(col, width)], cx_recv.at[i], cx_send.at[i], partner)

    bufs = [wqkv, wout]
    shard = [CORES * wr, CORES * wor]
    tails = [80, 32]

    def full(w, zz, xx):
        return bufs[w].at[at((zz * CHIPS_X + xx) * shard[w], shard[w])]

    def apart(w, zz, xx):
        return bufs[w].at[at((zz * CHIPS_X + xx) * shard[w], shard[w] - tails[w])]

    def bpart(w, zz, xx):
        return bufs[w].at[at((zz * CHIPS_X + xx + 1) * shard[w] - tails[w], tails[w])]

    can_up = z < PLANES - 1
    can_dn = z > 0

    def z_send(ref, w, t, part, up, cond):
        ss, rs = (up_send, up_recv) if up else (dn_send, dn_recv)
        target = z_up if up else z_dn
        send(ref, ref, ss.at[w, t, part], rs.at[w, t, part], target, cond)

    def x_send(ref, w, i, cond=None):
        send(ref, ref, xl_send.at[w, i], xl_recv.at[w, i], x_peer, cond)

    def gather_start(w):
        x_send(bpart(w, z, x), w, 0)
        z_send(full(w, z, x), w, 0, 0, True, can_up)
        z_send(full(w, z, x), w, 0, 0, False, can_dn)
        x_send(apart(w, z, x), w, 1)
        other = bpart(w, z, ox)
        arrived(other, xl_recv.at[w, 0], xl_send.at[w, 0], x_peer)
        z_send(other, w, 0, 1, True, can_up)
        z_send(other, w, 0, 1, False, can_dn)

    def gather_step(w, t):
        for up in (True, False):
            zz = z - t if up else z + t
            got = (z >= t) if up else (z + t <= PLANES - 1)
            on = got & (can_up if up else can_dn)
            zc = jnp.clip(zz, 0, PLANES - 1)
            ss, rs = (up_send, up_recv) if up else (dn_send, dn_recv)
            target = z_dn if up else z_up
            for part, ref in ((0, full(w, zc, x)), (1, bpart(w, zc, ox))):
                pl.when(got)(
                    lambda ref=ref, part=part: arrived(
                        ref, rs.at[w, t - 1, part], ss.at[w, t - 1, part], target
                    )
                )
                if t < PLANES - 1:
                    z_send(ref, w, t, part, up, on)
                if part == 0:
                    x_send(apart(w, zc, x), w, (1 if up else PLANES) + t, got)

    def gather_end(w):
        arrived(apart(w, z, ox), xl_recv.at[w, 1], xl_send.at[w, 1], x_peer)
        for t in range(1, PLANES):
            for up in (True, False):
                zz = z - t if up else z + t
                got = (z >= t) if up else (z + t <= PLANES - 1)
                zc = jnp.clip(zz, 0, PLANES - 1)
                i = (1 if up else PLANES) + t
                pl.when(got)(
                    lambda zc=zc, i=i: arrived(
                        apart(w, zc, ox), xl_recv.at[w, i], xl_send.at[w, i], x_peer
                    )
                )

    def norm(src):
        def body(i, carry):
            r = at(i * 32, 32, 32)
            wide = src[r, :].astype(jnp.float32)
            mean = jnp.mean(wide * wide, axis=-1, keepdims=True)
            hidden[r, :] = (wide * lax.rsqrt(mean + EPSILON) * gain_ref[...]).astype(jnp.bfloat16)
            return carry

        lax.fori_loop(0, tok // 32, body, 0)

    def make_mask(p):
        key_col = kcol_ref[p]
        def body(i, carry):
            r = at(i * 32, 32, 32)
            q_col = qcol_ref[p, r, :]
            shape = (32, seq_len)
            qi = chip * tok + i * 32 + lax.broadcasted_iota(jnp.int32, shape, 0)
            ki = lax.broadcasted_iota(jnp.int32, shape, 1)
            ok = (ki <= qi) & ((key_col == q_col) | (key_col == 0))
            mask[r, :] = jnp.where(ok, 0.0, -1e30).astype(jnp.float32)
            return carry

        lax.fori_loop(0, tok // 32, body, 0)

    tile = 3 * HEAD_DIM
    width_all = qh + 2 * kh

    def project(p, kv):
        def body(i, carry):
            cols = at(i * tile, tile, 128)
            acc[:, cols] = (
                jnp.dot(hidden[...], wqkv[:, cols], preferred_element_type=jnp.float32)
                + bias_ref[:, cols]
            )
            return carry

        lax.fori_loop(0, width_all // tile, body, 0)
        cosine, sine = cos_ref[p], sin_ref[p]

        def turn(u):
            return (u * cosine + pltpu.roll(u, HEAD_DIM // 2, 1) * sine).astype(jnp.bfloat16)

        own = at(chip * tok, tok)
        kv[own, pl.ds(0, HEAD_DIM)] = turn(acc[:, pl.ds(qh, HEAD_DIM)])
        kv[own, pl.ds(HEAD_DIM, HEAD_DIM)] = acc[:, pl.ds(qh + kh, HEAD_DIM)].astype(jnp.bfloat16)
        for step in range(1, CHIPS):
            target = (s, lax.rem(chip + step, CHIPS) * CORES + c)
            send(kv.at[own], kv.at[own], kv_send.at[p, step], kv_recv.at[p, step], target)

        def head(h, carry):
            qs[h] = turn(acc[:, at(h * HEAD_DIM, HEAD_DIM, 128)])
            return carry

        lax.fori_loop(0, group, head, 0)

    def keys_ready(p, kv):
        for step in range(1, CHIPS):
            origin = lax.rem(chip + CHIPS - step, CHIPS)
            arrived(
                kv.at[at(origin * tok, tok)], kv_recv.at[p, step], kv_send.at[p, step],
                (s, origin * CORES + c),
            )

    factor = HEAD_DIM ** (-0.5) * math.log2(math.e)

    def attend(kv, ctx, lo, hi):
        def head(h, carry):
            scores = lax.dot_general(
                qs[h], kv[:, pl.ds(0, HEAD_DIM)], (((1,), (1,)), ((), ())),
                preferred_element_type=jnp.float32,
            )
            scores = scores * factor + mask[...]
            probs = jnp.exp2(scores - jnp.max(scores, axis=-1, keepdims=True))
            total = jnp.sum(probs, axis=-1, keepdims=True)
            summed = jnp.dot(
                probs.astype(jnp.bfloat16), kv[:, pl.ds(HEAD_DIM, HEAD_DIM)],
                preferred_element_type=jnp.float32,
            )
            ctx[:, at(c * qh + h * HEAD_DIM, HEAD_DIM, 128)] = (summed / total).astype(jnp.bfloat16)
            return carry

        lax.fori_loop(lo, hi, head, 0)

    def share_ctx(p, ctx):
        ref = ctx.at[:, at(c * qh, qh, 128)]
        send(ref, ref, cx_send.at[6 + p], cx_recv.at[6 + p], partner)

    def ctx_ready(p, ctx):
        arrived(ctx.at[:, at(oc * qh, qh, 128)], cx_recv.at[6 + p], cx_send.at[6 + p], partner)

    def project_out(src, ctx, half):
        def body(i, carry):
            cols = at(i * 256, 256, 256)
            wide = src[:, at(c * oh + i * 256, 256, 256)].astype(jnp.float32)
            half[:, cols] = (
                wide + jnp.dot(ctx[...], wout[:, cols], preferred_element_type=jnp.float32)
            ).astype(jnp.bfloat16)
            return carry

        lax.fori_loop(0, oh // 256, body, 0)

    def give(p, half, out):
        cols = at(c * oh, oh, 128)
        send(
            half.at[at(oc * rows, rows)], out.at[:, cols], cx_send.at[8 + p], cx_recv.at[8 + p],
            partner,
        )
        copy = pltpu.make_async_copy(half.at[mine], out.at[:, cols], loc_sem.at[6 + p])
        copy.start()
        return copy

    def given(p, out):
        arrived(out.at[:, at(oc * oh, oh, 128)], cx_recv.at[8 + p], cx_send.at[8 + p], partner)

    for i in range(3):
        own_ready(i)
    gather_start(0)
    local[4].wait()
    other_rows = at(oc * rows, rows)
    arrived(xs1.at[other_rows], cx_recv.at[4], cx_send.at[4], partner)
    norm(xs1)
    gather_step(0, 1)
    make_mask(0)
    own_ready(3)
    gather_start(1)
    gather_step(0, 2)
    gather_step(0, 3)
    gather_end(0)
    gather_step(1, 1)
    project(0, kv1)
    gather_step(1, 2)
    keys_ready(0, kv1)
    attend(kv1, ctx1, 0, 3)
    gather_step(1, 3)
    attend(kv1, ctx1, 3, group)
    share_ctx(0, ctx1)
    make_mask(1)
    ctx_ready(0, ctx1)
    gather_end(1)
    project_out(xs1, ctx1, half1)

    my_cols = at(c * oh, oh, 128)
    send(half1, xs2.at[:, my_cols], ps_send.at[0], ps_recv.at[0], s_next, has_next)
    out_copy1 = give(0, half1, out1_ref)

    def from_first():
        inc_copy.wait()
        arrived(xs2.at[other_rows], cx_recv.at[5], cx_send.at[5], partner)

    pl.when(first)(from_first)
    cols_ref = xs2.at[:, my_cols]
    pl.when(has_prev)(
        lambda: arrived(cols_ref, ps_recv.at[0], ps_send.at[0], s_prev)
    )
    send(cols_ref, cols_ref, cx_send.at[10], cx_recv.at[10], partner, has_prev)
    pl.when(has_prev)(
        lambda: arrived(
            xs2.at[:, at(oc * oh, oh, 128)], cx_recv.at[10], cx_send.at[10], partner
        )
    )
    norm(xs2)
    project(1, kv2)
    keys_ready(1, kv2)
    attend(kv2, ctx2, 0, group)
    share_ctx(1, ctx2)
    ctx_ready(1, ctx2)
    project_out(xs2, ctx2, half2)
    out_copy2 = give(1, half2, out2_ref)

    given(0, out1_ref)
    given(1, out2_ref)
    out_copy1.wait()
    out_copy2.wait()
    for copy, cond in sent:
        if cond is None:
            copy.wait_send()
        else:
            pl.when(cond)(copy.wait_send)


def per_device(
    n_section,
    activations,
    incoming,
    column_ids,
    positions,
    norm_gain,
    w_query,
    w_key,
    w_value,
    w_out,
    b_query,
    b_key,
    b_value,
):
    _, rows, d = activations.shape
    qw, kvw = w_query.shape[2], w_key.shape[2]
    qh, kh, oh = qw // CORES, kvw // CORES, d // CORES
    tok = rows * CORES
    seq_len = column_ids.shape[1]
    s = lax.axis_index("section")
    me = lax.axis_index("seq")
    chip, core = me // CORES, me % CORES
    second_row = (s + n_section) % (n_section + 1)
    picked = jnp.stack([s, second_row])
    columns = jnp.take(column_ids, picked, axis=0, mode="clip")
    places = jnp.take(positions, picked, axis=0, mode="clip")
    q_cols = lax.dynamic_slice_in_dim(columns, chip * tok, tok, 1)[:, :, None]
    places = lax.dynamic_slice_in_dim(places, chip * tok, tok, 1).astype(jnp.float32)
    half = HEAD_DIM // 2
    freqs = THETA ** (-(jnp.arange(half, dtype=jnp.float32) * 2.0) / HEAD_DIM)
    angles = places[:, :, None] * freqs
    cosine, sine = jnp.cos(angles), jnp.sin(angles)
    cosine = jnp.concatenate([cosine, cosine], axis=-1)
    sine = jnp.concatenate([-sine, sine], axis=-1)
    bias = jnp.concatenate(
        [
            lax.dynamic_slice_in_dim(b_query, core * qh, qh, 1),
            lax.dynamic_slice_in_dim(b_key, core * kh, kh, 1),
            lax.dynamic_slice_in_dim(b_value, core * kh, kh, 1),
        ],
        axis=1,
    )
    bf16, f32 = jnp.bfloat16, jnp.float32
    anywhere = pl.BlockSpec(memory_space=pl.ANY)
    vmem = pl.BlockSpec(memory_space=pltpu.VMEM)
    dma = pltpu.SemaphoreType.DMA
    shape = jax.ShapeDtypeStruct((rows, d), bf16)
    width = qh + 2 * kh
    z_sems = dma((2, PLANES - 1, 2))
    out1, out2 = pl.pallas_call(
        functools.partial(kernel, n_section, (rows, d, qw, kvw)),
        out_shape=(shape, shape),
        in_specs=[anywhere] * 6 + [vmem] * 6,
        out_specs=(anywhere, anywhere),
        scratch_shapes=[
            pltpu.VMEM((d, width), bf16),
            pltpu.VMEM((qw, oh), bf16),
            pltpu.VMEM((tok, d), bf16),
            pltpu.VMEM((tok, d), bf16),
            pltpu.VMEM((tok, d), bf16),
            pltpu.VMEM((tok, width), f32),
            pltpu.VMEM((HEADS // KV_HEADS, tok, HEAD_DIM), bf16),
            pltpu.VMEM((seq_len, 2 * HEAD_DIM), bf16),
            pltpu.VMEM((seq_len, 2 * HEAD_DIM), bf16),
            pltpu.VMEM((tok, seq_len), f32),
            pltpu.VMEM((tok, qw), bf16),
            pltpu.VMEM((tok, qw), bf16),
            pltpu.VMEM((tok, oh), bf16),
            pltpu.VMEM((tok, oh), bf16),
            dma((8,)),
            dma((11,)),
            dma((11,)),
            z_sems,
            z_sems,
            z_sems,
            z_sems,
            dma((2, 2 * PLANES)),
            dma((2, 2 * PLANES)),
            dma((2, CHIPS)),
            dma((2, CHIPS)),
            dma((1,)),
            dma((1,)),
        ],
        compiler_params=pltpu.CompilerParams(
            collective_id=0, has_side_effects=True, vmem_limit_bytes=56 * 1024 * 1024
        ),
        name="two_sections",
    )(
        activations[0],
        incoming,
        w_query[0],
        w_key[0],
        w_value[0],
        w_out[0],
        norm_gain,
        bias,
        cosine,
        sine,
        q_cols,
        columns[:, None, :],
    )
    return (out1[None], out2[None])


def solution(mesh):
    placed = (
        P("section", "seq", None),
        P("seq", None),
        P(),
        P(),
        P("section", None),
        P("section", "seq", None),
        P("section", "seq", None),
        P("section", "seq", None),
        P("section", "seq", None),
        P("section", None),
        P("section", None),
        P("section", None),
    )
    return jax.shard_map(
        functools.partial(per_device, mesh.shape["section"]),
        mesh=mesh,
        in_specs=placed,
        out_specs=(P("section", "seq", None), P("section", "seq", None)),
        check_vma=False,
    )
```

```python
import functools
import math

import jax
import jax.numpy as jnp
from jax import lax
from jax.experimental import pallas as pl
from jax.experimental.pallas import tpu as pltpu
from jax.sharding import PartitionSpec as P

HEAD_DIM = 128
HEADS = 14
KV_HEADS = 2
EPSILON = 1e-06
THETA = 1000000.0
MESH = pl.DeviceIdType.MESH

PLANES, CHIPS_X, CORES = 4, 2, 2
CHIPS = PLANES * CHIPS_X


def kernel(
    n_section,
    dims,
    x_ref,
    inc_ref,
    wq_ref,
    wk_ref,
    wv_ref,
    wo_ref,
    gain_ref,
    bq_ref,
    bk_ref,
    bv_ref,
    freq_ref,
    cols_ref,
    pos_ref,
    out1_ref,
    out2_ref,
    wqkv,
    wout_a,
    wout_b,
    wout_c,
    xs1,
    xs2,
    hidden,
    acc,
    squares,
    turns,
    q_cols,
    qs,
    kv1,
    kv2,
    mask,
    ctx1,
    ctx2,
    half1,
    half2,
    loc_sem,
    cx_send,
    cx_recv,
    up_send,
    up_recv,
    dn_send,
    dn_recv,
    xl_send,
    xl_recv,
    kv_send,
    kv_recv,
    ps_send,
    ps_recv,
):
    (rows, d, qw, kvw) = dims
    seq_len = rows * CHIPS * CORES
    tok = rows * CORES
    qh, kh, oh = qw // CORES, kvw // CORES, d // CORES
    group = HEADS // KV_HEADS
    wr, wor = wq_ref.shape[0], wo_ref.shape[0]

    s = lax.axis_index("section")
    me = lax.axis_index("seq")
    chip = me // CORES
    c = me % CORES
    z = chip // CHIPS_X
    x = chip % CHIPS_X
    oc = 1 - c
    ox = 1 - x

    def dev(zz, xx, cc):
        return (s, (zz * CHIPS_X + xx) * CORES + cc)

    partner = dev(z, x, oc)
    x_peer = dev(z, ox, c)
    z_up = dev(jnp.minimum(z + 1, PLANES - 1), x, c)
    z_dn = dev(jnp.maximum(z - 1, 0), x, c)

    sent = []

    def send(src, dst, ssem, rsem, target, cond=None):
        copy = pltpu.make_async_remote_copy(
            src_ref=src, dst_ref=dst, send_sem=ssem, recv_sem=rsem,
            device_id=target, device_id_type=MESH,
        )
        if cond is None:
            copy.start()
        else:
            pl.when(cond)(copy.start)
        sent.append((copy, cond))

    def arrived(ref, rsem, ssem, target):
        pltpu.make_async_remote_copy(
            src_ref=ref, dst_ref=ref, send_sem=ssem, recv_sem=rsem,
            device_id=target, device_id_type=MESH,
        ).wait_recv()

    def at(offset, size, unit=16):
        return pl.ds(pl.multiple_of(offset, unit), size)

    kv1[...] = jnp.zeros_like(kv1)
    kv2[...] = jnp.zeros_like(kv2)

    barrier = pltpu.get_barrier_semaphore()

    def greet(target):
        pl.semaphore_signal(barrier, inc=1, device_id=target, device_id_type=MESH)

    greet(partner)
    greet(x_peer)
    can_up = z < PLANES - 1
    can_dn = z > 0
    pl.when(can_up)(lambda: greet(z_up))
    pl.when(can_dn)(lambda: greet(z_dn))
    has_prev = s > 0
    has_next = s < n_section - 1
    s_prev = (jnp.maximum(s - 1, 0), me)
    s_next = (jnp.minimum(s + 1, n_section - 1), me)
    pl.when(has_prev)(lambda: greet(s_prev))
    pl.when(has_next)(lambda: greet(s_next))
    peers = 2
    for there in (can_up, can_dn, has_prev, has_next):
        peers = peers + there.astype(jnp.int32)
    pl.semaphore_wait(barrier, peers)

    row0 = chip * (CORES * wr) + c * wr
    orow0 = chip * (CORES * wr) + oc * wr
    wrow0 = chip * (CORES * wor) + c * wor
    worow0 = chip * (CORES * wor) + oc * wor
    wouts = [wout_a, wout_b, wout_c]
    chunks = []
    low = 0
    for buf in wouts:
        chunks.append((low, buf.shape[1]))
        low += buf.shape[1]
    pieces = [
        (wq_ref, wqkv, row0, orow0, wr, qh, 0, 0),
        (wk_ref, wqkv, row0, orow0, wr, kh, 0, qh),
        (wv_ref, wqkv, row0, orow0, wr, kh, 0, qh + kh),
    ] + [
        (wo_ref, buf, wrow0, worow0, wor, oh, lo, 0) for buf, (lo, _) in zip(wouts, chunks)
    ]
    widths = [qh, kh, kh] + [w for _, w in chunks]
    local = []
    for i, (src, dst, r0, _, n, part, lo, col) in enumerate(pieces):
        width = widths[i]
        there = dst.at[at(r0, n), pl.ds(col, width)]
        send(
            src.at[:, at(oc * part + lo, width, 128)], there, cx_send.at[i], cx_recv.at[i], partner
        )
        copy = pltpu.make_async_copy(
            src.at[:, at(c * part + lo, width, 128)], there, loc_sem.at[i]
        )
        copy.start()
        local.append(copy)

    mine = at(c * rows, rows)
    send(x_ref, xs1.at[mine], cx_send.at[6], cx_recv.at[6], partner)
    copy = pltpu.make_async_copy(x_ref, xs1.at[mine], loc_sem.at[6])
    copy.start()
    local.append(copy)
    first = s == 0
    send(inc_ref, xs2.at[mine], cx_send.at[7], cx_recv.at[7], partner, first)
    inc_copy = pltpu.make_async_copy(inc_ref, xs2.at[mine], loc_sem.at[7])
    pl.when(first)(inc_copy.start)

    def own_ready(i):
        _, dst, _, r1, n, _, _, col = pieces[i]
        local[i].wait()
        arrived(dst.at[at(r1, n), pl.ds(col, widths[i])], cx_recv.at[i], cx_send.at[i], partner)

    bufs = [wqkv] + wouts
    shard = [CORES * wr] + [CORES * wor] * len(wouts)
    tails = [80] + [32] * len(wouts)

    def apart(w, zz, xx):
        return bufs[w].at[at((zz * CHIPS_X + xx) * shard[w], shard[w] - tails[w])]

    def bpart(w, zz, xx):
        return bufs[w].at[at((zz * CHIPS_X + xx + 1) * shard[w] - tails[w], tails[w])]

    def z_send(ref, w, t, part, up, cond):
        ss, rs = (up_send, up_recv) if up else (dn_send, dn_recv)
        target = z_up if up else z_dn
        send(ref, ref, ss.at[w, t, part], rs.at[w, t, part], target, cond)

    def x_send(ref, w, i, cond=None):
        send(ref, ref, xl_send.at[w, i], xl_recv.at[w, i], x_peer, cond)

    def flow(up, t):
        zz = z - t if up else z + t
        got = (z >= t) if up else (z + t <= PLANES - 1)
        on = got & (can_up if up else can_dn)
        return jnp.clip(zz, 0, PLANES - 1), got, on

    def a_start(w):
        x_send(bpart(w, z, x), w, 0)
        z_send(apart(w, z, x), w, 0, 0, True, can_up)
        z_send(apart(w, z, x), w, 0, 0, False, can_dn)
        x_send(apart(w, z, x), w, 1)

    def b_start(w):
        other = bpart(w, z, ox)
        arrived(other, xl_recv.at[w, 0], xl_send.at[w, 0], x_peer)
        for part, ref in ((1, bpart(w, z, x)), (2, other)):
            z_send(ref, w, 0, part, True, can_up)
            z_send(ref, w, 0, part, False, can_dn)

    def z_arrived(ref, w, t, part, up, got):
        ss, rs = (up_send, up_recv) if up else (dn_send, dn_recv)
        target = z_dn if up else z_up
        pl.when(got)(
            lambda: arrived(ref, rs.at[w, t - 1, part], ss.at[w, t - 1, part], target)
        )

    def a_step(w, t):
        for up in (True, False):
            zc, got, on = flow(up, t)
            ref = apart(w, zc, x)
            z_arrived(ref, w, t, 0, up, got)
            if t < PLANES - 1:
                z_send(ref, w, t, 0, up, on)
            x_send(ref, w, (1 if up else PLANES) + t, got)

    def b_step(w, t):
        for up in (True, False):
            zc, got, on = flow(up, t)
            for part, ref in ((1, bpart(w, zc, x)), (2, bpart(w, zc, ox))):
                z_arrived(ref, w, t, part, up, got)
                if t < PLANES - 1:
                    z_send(ref, w, t, part, up, on)

    def b_steps(w):
        for t in range(1, PLANES):
            b_step(w, t)

    def gather_end(w):
        arrived(apart(w, z, ox), xl_recv.at[w, 1], xl_send.at[w, 1], x_peer)
        for t in range(1, PLANES):
            for up in (True, False):
                zc, got, _ = flow(up, t)
                i = (1 if up else PLANES) + t
                pl.when(got)(
                    lambda zc=zc, i=i: arrived(
                        apart(w, zc, ox), xl_recv.at[w, i], xl_send.at[w, i], x_peer
                    )
                )

    micro = [s, lax.rem(s + n_section, n_section + 1)]

    def tables(p):
        own = at(chip * tok, tok, 128)
        eye = lax.broadcasted_iota(jnp.int32, (tok, tok), 0) == lax.broadcasted_iota(
            jnp.int32, (tok, tok), 1
        )

        def upright(ref):
            entries = ref[pl.ds(micro[p], 1), own].astype(jnp.float32)
            return jnp.sum(jnp.where(eye, entries, 0.0), axis=1, keepdims=True)

        q_cols[p] = jnp.broadcast_to(upright(cols_ref), (tok, HEAD_DIM))
        angles = upright(pos_ref) * freq_ref[0:1, :]
        turns[p, 0] = jnp.cos(angles)
        turns[p, 1] = jnp.sin(angles) * freq_ref[1:2, :]

    def make_mask(p):
        key_col = cols_ref[pl.ds(micro[p], 1), :].astype(jnp.float32)

        def body(i, carry):
            r = at(i * 32, 32, 32)
            q_col = q_cols[p, r, 0:1]
            shape = (32, seq_len)
            qi = chip * tok + i * 32 + lax.broadcasted_iota(jnp.int32, shape, 0)
            ki = lax.broadcasted_iota(jnp.int32, shape, 1)
            ok = (ki <= qi) & ((key_col == q_col) | (key_col == 0.0))
            mask[r, :] = jnp.where(ok, 0.0, -1e30).astype(jnp.float32)
            return carry

        lax.fori_loop(0, tok // 32, body, 0)

    def scale_in(src, lo, width, start):
        def body(i, carry):
            r = at(i * 32, 32, 32)
            total = jnp.zeros((32, 1), jnp.float32)
            for cc in range(CORES):
                cols = pl.ds(cc * oh + lo, width)
                wide = src[r, cols].astype(jnp.float32)
                hidden[r, cols] = (wide * gain_ref[:, cols]).astype(jnp.bfloat16)
                total += jnp.sum(wide * wide, axis=-1, keepdims=True)
            total = jnp.broadcast_to(total, (32, HEAD_DIM))
            squares[r, :] = total if start else squares[r, :] + total
            return carry

        lax.fori_loop(0, tok // 32, body, 0)

    def multiply(lo, width, col, n, start):
        total = 0.0
        for cc in range(CORES):
            part = pl.ds(cc * oh + lo, width)
            total += jnp.dot(
                hidden[:, part], wqkv[part, pl.ds(col, n)], preferred_element_type=jnp.float32
            )
        cols = pl.ds(col, n)
        acc[:, cols] = total if start else acc[:, cols] + total

    def row_factor():
        return lax.rsqrt(squares[...] * (1.0 / d) + EPSILON)

    def turn(p, u):
        return (u * turns[p, 0] + pltpu.roll(u, HEAD_DIM // 2, 1) * turns[p, 1]).astype(
            jnp.bfloat16
        )

    def kv_rows(kv, zz, xx):
        return kv.at[at((zz * CHIPS_X + xx) * tok, tok)]

    def kv_x_send(p, ref, i, cond):
        send(ref, ref, kv_send.at[p, 1, i], kv_recv.at[p, 1, i], x_peer, cond)

    def kv_z_send(p, ref, i, cond):
        send(ref, ref, kv_send.at[p, 0, i], kv_recv.at[p, 0, i], z_up, cond)

    def finish_keys(p, kv):
        factor = row_factor()
        own = at(chip * tok, tok)
        key_bias = bk_ref[:, at(c * kh, kh, 128)]
        value_bias = bv_ref[:, at(c * kh, kh, 128)]
        kv[own, pl.ds(0, kh)] = turn(p, acc[:, pl.ds(qh, kh)] * factor + key_bias)
        kv[own, pl.ds(kh, kh)] = (acc[:, pl.ds(qh + kh, kh)] * factor + value_bias).astype(
            jnp.bfloat16
        )
        mine_kv = kv_rows(kv, z, x)
        kv_z_send(p, mine_kv, 0, can_up)
        kv_x_send(p, mine_kv, 0, x < ox)

    def finish_queries(p):
        factor = row_factor()

        def head(h, carry):
            cols = at(h * HEAD_DIM, HEAD_DIM, 128)
            query_bias = bq_ref[:, at(c * qh + h * HEAD_DIM, HEAD_DIM, 128)]
            qs[h] = turn(p, acc[:, cols] * factor + query_bias)
            return carry

        lax.fori_loop(0, group, head, 0)

    def kv_step(p, kv, t):
        zc, got, on = flow(True, t)
        ref = kv_rows(kv, zc, x)
        pl.when(got)(
            lambda: arrived(ref, kv_recv.at[p, 0, t - 1], kv_send.at[p, 0, t - 1], z_dn)
        )
        if t < PLANES - 1:
            kv_z_send(p, ref, t, on)
        kv_x_send(p, ref, t, got)

    def keys_ready(p, kv):
        for t in range(PLANES):
            zc, got, _ = flow(True, t)
            pl.when(got if t else x > ox)(
                lambda zc=zc, t=t: arrived(
                    kv_rows(kv, zc, ox), kv_recv.at[p, 1, t], kv_send.at[p, 1, t], x_peer
                )
            )

    exp_factor = HEAD_DIM ** (-0.5) * math.log2(math.e)

    def attend(kv, ctx, lo, hi):
        def head(h, carry):
            scores = lax.dot_general(
                qs[h], kv[:, pl.ds(0, HEAD_DIM)], (((1,), (1,)), ((), ())),
                preferred_element_type=jnp.float32,
            )
            scores = scores * exp_factor + mask[...]
            probs = jnp.exp2(scores - jnp.max(scores, axis=-1, keepdims=True))
            total = jnp.sum(probs, axis=-1, keepdims=True)
            summed = jnp.dot(
                probs.astype(jnp.bfloat16), kv[:, pl.ds(HEAD_DIM, HEAD_DIM)],
                preferred_element_type=jnp.float32,
            )
            ctx[:, at(c * qh + h * HEAD_DIM, HEAD_DIM, 128)] = (summed / total).astype(jnp.bfloat16)
            return carry

        lax.fori_loop(lo, hi, head, 0)

    def share_ctx(p, ctx):
        ref = ctx.at[:, at(c * qh, qh, 128)]
        send(ref, ref, cx_send.at[8 + p], cx_recv.at[8 + p], partner)

    def ctx_ready(p, ctx):
        arrived(ctx.at[:, at(oc * qh, qh, 128)], cx_recv.at[8 + p], cx_send.at[8 + p], partner)

    def project_out(src, ctx, half, j):
        lo, width = chunks[j]
        wide = src[:, at(c * oh + lo, width, 128)].astype(jnp.float32)
        half[:, pl.ds(lo, width)] = (
            wide + jnp.dot(ctx[...], wouts[j][...], preferred_element_type=jnp.float32)
        ).astype(jnp.bfloat16)

    def give(p, half, out):
        cols = at(c * oh, oh, 128)
        send(
            half.at[at(oc * rows, rows)], out.at[:, cols], cx_send.at[10 + p], cx_recv.at[10 + p],
            partner,
        )
        copy = pltpu.make_async_copy(half.at[mine], out.at[:, cols], loc_sem.at[8 + p])
        copy.start()
        return copy

    def given(p, out):
        arrived(out.at[:, at(oc * oh, oh, 128)], cx_recv.at[10 + p], cx_send.at[10 + p], partner)

    def pass_on(j):
        lo, width = chunks[j]
        send(
            half1.at[:, pl.ds(lo, width)], xs2.at[:, at(c * oh + lo, width, 128)],
            ps_send.at[j], ps_recv.at[j], s_next, has_next,
        )

    def passed(j):
        lo, width = chunks[j]
        ref = xs2.at[:, at(c * oh + lo, width, 128)]
        pl.when(has_prev)(lambda: arrived(ref, ps_recv.at[j], ps_send.at[j], s_prev))
        send(ref, ref, cx_send.at[12 + j], cx_recv.at[12 + j], partner, has_prev)
        pl.when(has_prev)(
            lambda: arrived(
                xs2.at[:, at(oc * oh + lo, width, 128)], cx_recv.at[12 + j], cx_send.at[12 + j],
                partner,
            )
        )
        scale_in(xs2, lo, width, j == 0)

    for i in range(3):
        own_ready(i)
    a_start(0)
    tables(0)
    tables(1)
    make_mask(0)
    local[6].wait()
    other_rows = at(oc * rows, rows)
    arrived(xs1.at[other_rows], cx_recv.at[6], cx_send.at[6], partner)
    scale_in(xs1, 0, oh, True)
    for i in range(3, len(pieces)):
        own_ready(i)

    def from_first():
        inc_copy.wait()
        arrived(xs2.at[other_rows], cx_recv.at[7], cx_send.at[7], partner)

    pl.when(first)(from_first)
    a_step(0, 1)
    a_step(0, 2)
    a_start(1)
    a_step(0, 3)
    b_start(0)
    b_steps(0)
    a_step(1, 1)
    gather_end(0)
    multiply(0, oh, qh, 2 * kh, True)
    finish_keys(0, kv1)
    multiply(0, oh, 0, qh, True)
    finish_queries(0)
    a_step(1, 2)
    a_start(2)
    a_step(1, 3)
    b_start(1)
    b_steps(1)
    for t in range(1, PLANES):
        kv_step(0, kv1, t)
    a_step(2, 1)
    keys_ready(0, kv1)
    attend(kv1, ctx1, 0, 3)
    a_step(2, 2)
    a_start(3)
    attend(kv1, ctx1, 3, group)
    share_ctx(0, ctx1)
    a_step(2, 3)
    b_start(2)
    b_steps(2)
    a_step(3, 1)
    make_mask(1)
    ctx_ready(0, ctx1)
    gather_end(1)
    project_out(xs1, ctx1, half1, 0)
    pass_on(0)
    a_step(3, 2)
    a_step(3, 3)
    b_start(3)
    gather_end(2)
    project_out(xs1, ctx1, half1, 1)
    pass_on(1)
    passed(0)
    multiply(*chunks[0], qh, 2 * kh, True)
    multiply(*chunks[0], 0, qh, True)
    b_steps(3)
    passed(1)
    multiply(*chunks[1], qh, 2 * kh, False)
    multiply(*chunks[1], 0, qh, False)
    gather_end(3)
    project_out(xs1, ctx1, half1, 2)
    pass_on(2)
    out_copy1 = give(0, half1, out1_ref)
    passed(2)
    multiply(*chunks[2], qh, 2 * kh, False)
    finish_keys(1, kv2)
    multiply(*chunks[2], 0, qh, False)
    finish_queries(1)
    for t in range(1, PLANES):
        kv_step(1, kv2, t)
    keys_ready(1, kv2)
    attend(kv2, ctx2, 0, group)
    share_ctx(1, ctx2)
    ctx_ready(1, ctx2)
    for j in range(len(chunks)):
        project_out(xs2, ctx2, half2, j)
    out_copy2 = give(1, half2, out2_ref)

    given(0, out1_ref)
    given(1, out2_ref)
    out_copy1.wait()
    out_copy2.wait()
    for copy, cond in sent:
        if cond is None:
            copy.wait_send()
        else:
            pl.when(cond)(copy.wait_send)


def per_device(
    n_section,
    activations,
    incoming,
    column_ids,
    positions,
    norm_gain,
    w_query,
    w_key,
    w_value,
    w_out,
    b_query,
    b_key,
    b_value,
):
    _, rows, d = activations.shape
    qw, kvw = w_query.shape[2], w_key.shape[2]
    qh, kh, oh = qw // CORES, kvw // CORES, d // CORES
    tok = rows * CORES
    seq_len = column_ids.shape[1]
    half = HEAD_DIM // 2
    freqs = THETA ** (-(jnp.arange(half, dtype=jnp.float32) * 2.0) / HEAD_DIM)
    signs = jnp.ones((half,), jnp.float32)
    freqs = jnp.stack([jnp.concatenate([freqs, freqs]), jnp.concatenate([-signs, signs])])
    cuts = [oh * 3 // 7, oh * 5 // 14, oh * 3 // 14]
    bf16, f32 = jnp.bfloat16, jnp.float32
    anywhere = pl.BlockSpec(memory_space=pl.ANY)
    vmem = pl.BlockSpec(memory_space=pltpu.VMEM)
    dma = pltpu.SemaphoreType.DMA
    shape = jax.ShapeDtypeStruct((rows, d), bf16)
    width = qh + 2 * kh
    jobs = 1 + len(cuts)
    z_sems = dma((jobs, PLANES - 1, 3))
    out1, out2 = pl.pallas_call(
        functools.partial(kernel, n_section, (rows, d, qw, kvw)),
        out_shape=(shape, shape),
        in_specs=[anywhere] * 6 + [vmem] * 7,
        out_specs=(anywhere, anywhere),
        scratch_shapes=[
            pltpu.VMEM((d, width), bf16),
            *[pltpu.VMEM((qw, cut), bf16) for cut in cuts],
            pltpu.VMEM((tok, d), bf16),
            pltpu.VMEM((tok, d), bf16),
            pltpu.VMEM((tok, d), bf16),
            pltpu.VMEM((tok, width), f32),
            pltpu.VMEM((tok, HEAD_DIM), f32),
            pltpu.VMEM((2, 2, tok, HEAD_DIM), f32),
            pltpu.VMEM((2, tok, HEAD_DIM), f32),
            pltpu.VMEM((HEADS // KV_HEADS, tok, HEAD_DIM), bf16),
            pltpu.VMEM((seq_len, 2 * HEAD_DIM), bf16),
            pltpu.VMEM((seq_len, 2 * HEAD_DIM), bf16),
            pltpu.VMEM((tok, seq_len), f32),
            pltpu.VMEM((tok, qw), bf16),
            pltpu.VMEM((tok, qw), bf16),
            pltpu.VMEM((tok, oh), bf16),
            pltpu.VMEM((tok, oh), bf16),
            dma((10,)),
            dma((15,)),
            dma((15,)),
            z_sems,
            z_sems,
            z_sems,
            z_sems,
            dma((jobs, 2 * PLANES)),
            dma((jobs, 2 * PLANES)),
            dma((2, 2, PLANES)),
            dma((2, 2, PLANES)),
            dma((len(cuts),)),
            dma((len(cuts),)),
        ],
        compiler_params=pltpu.CompilerParams(
            collective_id=0, has_side_effects=True, vmem_limit_bytes=56 * 1024 * 1024
        ),
        name="two_sections",
    )(
        activations[0],
        incoming,
        w_query[0],
        w_key[0],
        w_value[0],
        w_out[0],
        norm_gain,
        b_query,
        b_key,
        b_value,
        freqs,
        column_ids,
        positions,
    )
    return (out1[None], out2[None])


def solution(mesh):
    placed = (
        P("section", "seq", None),
        P("seq", None),
        P(),
        P(),
        P("section", None),
        P("section", "seq", None),
        P("section", "seq", None),
        P("section", "seq", None),
        P("section", "seq", None),
        P("section", None),
        P("section", None),
        P("section", None),
    )
    return jax.shard_map(
        functools.partial(per_device, mesh.shape["section"]),
        mesh=mesh,
        in_specs=placed,
        out_specs=(P("section", "seq", None), P("section", "seq", None)),
        check_vma=False,
    )
```

```python
import functools
import math

import jax
import jax.numpy as jnp
from jax import lax
from jax.experimental import pallas as pl
from jax.experimental.pallas import tpu as pltpu
from jax.sharding import PartitionSpec as P

HEAD_DIM = 128
HEADS = 14
KV_HEADS = 2
EPSILON = 1e-06
THETA = 1000000.0
MESH = pl.DeviceIdType.MESH

PLANES, CHIPS_X, CORES = 4, 2, 2
CHIPS = PLANES * CHIPS_X


def kernel(
    n_section,
    dims,
    x_ref,
    inc_ref,
    wq_ref,
    wk_ref,
    wv_ref,
    wo_ref,
    gain_ref,
    bq_ref,
    bk_ref,
    bv_ref,
    freq_ref,
    cols_ref,
    pos_ref,
    out1_ref,
    out2_ref,
    wqkv,
    wout_a,
    wout_b,
    wout_c,
    xs1,
    xs2,
    hidden,
    acc,
    squares,
    turns,
    q_cols,
    qs,
    tops,
    sums,
    mixed,
    kv1,
    kv2,
    mask,
    ctx1,
    ctx2,
    half1,
    half2,
    partial,
    loc_sem,
    cx_send,
    cx_recv,
    up_send,
    up_recv,
    dn_send,
    dn_recv,
    xl_send,
    xl_recv,
    kv_send,
    kv_recv,
    ps_send,
    ps_recv,
):
    (rows, d, qw, kvw) = dims
    seq_len = rows * CHIPS * CORES
    tok = rows * CORES
    qh, kh, oh = qw // CORES, kvw // CORES, d // CORES
    group = HEADS // KV_HEADS
    wr, wor = wq_ref.shape[0], wo_ref.shape[0]

    s = lax.axis_index("section")
    me = lax.axis_index("seq")
    chip = me // CORES
    c = me % CORES
    z = chip // CHIPS_X
    x = chip % CHIPS_X
    oc = 1 - c
    ox = 1 - x

    def dev(zz, xx, cc):
        return (s, (zz * CHIPS_X + xx) * CORES + cc)

    partner = dev(z, x, oc)
    x_peer = dev(z, ox, c)
    z_up = dev(jnp.minimum(z + 1, PLANES - 1), x, c)
    z_dn = dev(jnp.maximum(z - 1, 0), x, c)

    sent = []

    def send(src, dst, ssem, rsem, target, cond=None):
        copy = pltpu.make_async_remote_copy(
            src_ref=src, dst_ref=dst, send_sem=ssem, recv_sem=rsem,
            device_id=target, device_id_type=MESH,
        )
        if cond is None:
            copy.start()
        else:
            pl.when(cond)(copy.start)
        sent.append((copy, cond))

    def arrived(ref, rsem, ssem, target):
        pltpu.make_async_remote_copy(
            src_ref=ref, dst_ref=ref, send_sem=ssem, recv_sem=rsem,
            device_id=target, device_id_type=MESH,
        ).wait_recv()

    def at(offset, size, unit=16):
        return pl.ds(pl.multiple_of(offset, unit), size)

    kv1[...] = jnp.zeros_like(kv1)
    kv2[...] = jnp.zeros_like(kv2)

    barrier = pltpu.get_barrier_semaphore()

    def greet(target):
        pl.semaphore_signal(barrier, inc=1, device_id=target, device_id_type=MESH)

    greet(partner)
    greet(x_peer)
    can_up = z < PLANES - 1
    can_dn = z > 0
    pl.when(can_up)(lambda: greet(z_up))
    pl.when(can_dn)(lambda: greet(z_dn))
    has_prev = s > 0
    has_next = s < n_section - 1
    s_prev = (jnp.maximum(s - 1, 0), me)
    s_next = (jnp.minimum(s + 1, n_section - 1), me)
    pl.when(has_prev)(lambda: greet(s_prev))
    pl.when(has_next)(lambda: greet(s_next))
    peers = 2
    for there in (can_up, can_dn, has_prev, has_next):
        peers = peers + there.astype(jnp.int32)
    pl.semaphore_wait(barrier, peers)

    row0 = chip * (CORES * wr) + c * wr
    orow0 = chip * (CORES * wr) + oc * wr
    wrow0 = chip * (CORES * wor) + c * wor
    worow0 = chip * (CORES * wor) + oc * wor
    wouts = [wout_a, wout_b, wout_c]
    chunks = []
    low = 0
    for buf in wouts:
        chunks.append((low, buf.shape[1]))
        low += buf.shape[1]
    pieces = [
        (wq_ref, wqkv, row0, orow0, wr, qh, 0, 0),
        (wk_ref, wqkv, row0, orow0, wr, kh, 0, qh),
        (wv_ref, wqkv, row0, orow0, wr, kh, 0, qh + kh),
    ] + [
        (wo_ref, buf, wrow0, worow0, wor, oh, lo, 0) for buf, (lo, _) in zip(wouts, chunks)
    ]
    widths = [qh, kh, kh] + [w for _, w in chunks]
    local = []
    for i, (src, dst, r0, _, n, part, lo, col) in enumerate(pieces):
        width = widths[i]
        there = dst.at[at(r0, n), pl.ds(col, width)]
        send(
            src.at[:, at(oc * part + lo, width, 128)], there, cx_send.at[i], cx_recv.at[i], partner
        )
        copy = pltpu.make_async_copy(
            src.at[:, at(c * part + lo, width, 128)], there, loc_sem.at[i]
        )
        copy.start()
        local.append(copy)

    mine = at(c * rows, rows)
    send(x_ref, xs1.at[mine], cx_send.at[6], cx_recv.at[6], partner)
    copy = pltpu.make_async_copy(x_ref, xs1.at[mine], loc_sem.at[6])
    copy.start()
    local.append(copy)
    first = s == 0
    send(inc_ref, xs2.at[mine], cx_send.at[7], cx_recv.at[7], partner, first)
    inc_copy = pltpu.make_async_copy(inc_ref, xs2.at[mine], loc_sem.at[7])
    pl.when(first)(inc_copy.start)

    def own_ready(i):
        _, dst, _, r1, n, _, _, col = pieces[i]
        local[i].wait()
        arrived(dst.at[at(r1, n), pl.ds(col, widths[i])], cx_recv.at[i], cx_send.at[i], partner)

    bufs = [wqkv] + wouts
    shard = [CORES * wr] + [CORES * wor] * len(wouts)
    tails = [80] + [32] * len(wouts)

    def apart(w, zz, xx):
        return bufs[w].at[at((zz * CHIPS_X + xx) * shard[w], shard[w] - tails[w])]

    def bpart(w, zz, xx):
        return bufs[w].at[at((zz * CHIPS_X + xx + 1) * shard[w] - tails[w], tails[w])]

    def z_send(ref, w, t, part, up, cond):
        ss, rs = (up_send, up_recv) if up else (dn_send, dn_recv)
        target = z_up if up else z_dn
        send(ref, ref, ss.at[w, t, part], rs.at[w, t, part], target, cond)

    def x_send(ref, w, i, cond=None):
        send(ref, ref, xl_send.at[w, i], xl_recv.at[w, i], x_peer, cond)

    def flow(up, t):
        zz = z - t if up else z + t
        got = (z >= t) if up else (z + t <= PLANES - 1)
        on = got & (can_up if up else can_dn)
        return jnp.clip(zz, 0, PLANES - 1), got, on

    def a_start(w):
        x_send(bpart(w, z, x), w, 0)
        z_send(apart(w, z, x), w, 0, 0, True, can_up)
        z_send(apart(w, z, x), w, 0, 0, False, can_dn)
        x_send(apart(w, z, x), w, 1)

    def b_start(w):
        other = bpart(w, z, ox)
        arrived(other, xl_recv.at[w, 0], xl_send.at[w, 0], x_peer)
        for part, ref in ((1, bpart(w, z, x)), (2, other)):
            z_send(ref, w, 0, part, True, can_up)
            z_send(ref, w, 0, part, False, can_dn)

    def z_arrived(ref, w, t, part, up, got):
        ss, rs = (up_send, up_recv) if up else (dn_send, dn_recv)
        target = z_dn if up else z_up
        pl.when(got)(
            lambda: arrived(ref, rs.at[w, t - 1, part], ss.at[w, t - 1, part], target)
        )

    def a_step(w, t):
        for up in (True, False):
            zc, got, on = flow(up, t)
            ref = apart(w, zc, x)
            z_arrived(ref, w, t, 0, up, got)
            if t < PLANES - 1:
                z_send(ref, w, t, 0, up, on)
            x_send(ref, w, (1 if up else PLANES) + t, got)

    def b_step(w, t):
        for up in (True, False):
            zc, got, on = flow(up, t)
            for part, ref in ((1, bpart(w, zc, x)), (2, bpart(w, zc, ox))):
                z_arrived(ref, w, t, part, up, got)
                if t < PLANES - 1:
                    z_send(ref, w, t, part, up, on)

    def b_steps(w):
        for t in range(1, PLANES):
            b_step(w, t)

    def gather_end(w):
        arrived(apart(w, z, ox), xl_recv.at[w, 1], xl_send.at[w, 1], x_peer)
        for t in range(1, PLANES):
            for up in (True, False):
                zc, got, _ = flow(up, t)
                i = (1 if up else PLANES) + t
                pl.when(got)(
                    lambda zc=zc, i=i: arrived(
                        apart(w, zc, ox), xl_recv.at[w, i], xl_send.at[w, i], x_peer
                    )
                )

    exp_factor = HEAD_DIM ** (-0.5) * math.log2(math.e)
    micro = [s, lax.rem(s + n_section, n_section + 1)]

    def tables(p):
        own = at(chip * tok, tok, 128)
        eye = lax.broadcasted_iota(jnp.int32, (tok, tok), 0) == lax.broadcasted_iota(
            jnp.int32, (tok, tok), 1
        )

        def upright(ref):
            entries = ref[pl.ds(micro[p], 1), own].astype(jnp.float32)
            return jnp.sum(jnp.where(eye, entries, 0.0), axis=1, keepdims=True)

        q_cols[p] = jnp.broadcast_to(upright(cols_ref), (tok, HEAD_DIM))
        angles = upright(pos_ref) * freq_ref[0:1, :]
        turns[p, 0] = jnp.cos(angles)
        turns[p, 1] = jnp.sin(angles) * freq_ref[1:2, :]

    def make_mask(p):
        key_col = cols_ref[pl.ds(micro[p], 1), :].astype(jnp.float32)

        def body(i, carry):
            r = at(i * 32, 32, 32)
            q_col = q_cols[p, r, 0:1]
            shape = (32, seq_len)
            qi = chip * tok + i * 32 + lax.broadcasted_iota(jnp.int32, shape, 0)
            ki = lax.broadcasted_iota(jnp.int32, shape, 1)
            ok = (ki <= qi) & ((key_col == q_col) | (key_col == 0.0))
            mask[r, :] = jnp.where(ok, 0.0, -1e30).astype(jnp.float32)
            return carry

        lax.fori_loop(0, tok // 32, body, 0)

    def scale_in(src, lo, width, start):
        def body(i, carry):
            r = at(i * 32, 32, 32)
            total = jnp.zeros((32, 1), jnp.float32)
            for cc in range(CORES):
                cols = pl.ds(cc * oh + lo, width)
                wide = src[r, cols].astype(jnp.float32)
                hidden[r, cols] = (wide * gain_ref[:, cols]).astype(jnp.bfloat16)
                total += jnp.sum(wide * wide, axis=-1, keepdims=True)
            total = jnp.broadcast_to(total, (32, HEAD_DIM))
            squares[r, :] = total if start else squares[r, :] + total
            return carry

        lax.fori_loop(0, tok // 32, body, 0)

    def multiply(lo, width, col, n, start):
        total = 0.0
        for cc in range(CORES):
            part = pl.ds(cc * oh + lo, width)
            total += jnp.dot(
                hidden[:, part], wqkv[part, pl.ds(col, n)], preferred_element_type=jnp.float32
            )
        cols = pl.ds(col, n)
        acc[:, cols] = total if start else acc[:, cols] + total

    def row_factor():
        return lax.rsqrt(squares[...] * (1.0 / d) + EPSILON)

    def turn(p, u):
        return u * turns[p, 0] + pltpu.roll(u, HEAD_DIM // 2, 1) * turns[p, 1]

    def kv_rows(kv, zz, xx):
        return kv.at[at((zz * CHIPS_X + xx) * tok, tok)]

    def kv_x_send(p, ref, i, cond):
        send(ref, ref, kv_send.at[p, 1, i], kv_recv.at[p, 1, i], x_peer, cond)

    def kv_z_send(p, ref, i, cond):
        send(ref, ref, kv_send.at[p, 0, i], kv_recv.at[p, 0, i], z_up, cond)

    def finish_keys(p, kv):
        factor = row_factor()
        own = at(chip * tok, tok)
        key_bias = bk_ref[:, at(c * kh, kh, 128)]
        value_bias = bv_ref[:, at(c * kh, kh, 128)]
        kv[own, pl.ds(0, kh)] = turn(p, acc[:, pl.ds(qh, kh)] * factor + key_bias).astype(
            jnp.bfloat16
        )
        kv[own, pl.ds(kh, kh)] = (acc[:, pl.ds(qh + kh, kh)] * factor + value_bias).astype(
            jnp.bfloat16
        )
        mine_kv = kv_rows(kv, z, x)
        kv_z_send(p, mine_kv, 0, can_up)
        kv_x_send(p, mine_kv, 0, x < ox)

    def finish_queries(p):
        factor = row_factor()

        def head(h, carry):
            cols = at(h * HEAD_DIM, HEAD_DIM, 128)
            query_bias = bq_ref[:, at(c * qh + h * HEAD_DIM, HEAD_DIM, 128)]
            turned = turn(p, acc[:, cols] * factor + query_bias)
            qs[h] = (turned * exp_factor).astype(jnp.bfloat16)
            return carry

        lax.fori_loop(0, group, head, 0)

    def kv_step(p, kv, t):
        zc, got, on = flow(True, t)
        ref = kv_rows(kv, zc, x)
        pl.when(got)(
            lambda: arrived(ref, kv_recv.at[p, 0, t - 1], kv_send.at[p, 0, t - 1], z_dn)
        )
        if t < PLANES - 1:
            kv_z_send(p, ref, t, on)
        kv_x_send(p, ref, t, got)

    plane = CHIPS_X * tok

    def attend(p, kv, t):
        zc, got, _ = flow(True, t)
        peer_keys = lambda: arrived(
            kv_rows(kv, zc, ox), kv_recv.at[p, 1, t], kv_send.at[p, 1, t], x_peer
        )

        def head(h, carry):
            rows_in = at(zc * plane, plane, 128)
            scores = lax.dot_general(
                qs[h], kv[rows_in, pl.ds(0, HEAD_DIM)], (((1,), (1,)), ((), ())),
                preferred_element_type=jnp.float32,
            )
            scores = scores + mask[:, rows_in]
            top = jnp.max(scores, axis=-1, keepdims=True)
            wide = (tok, HEAD_DIM)
            if t:
                top = jnp.maximum(top, tops[h, :, 0:1])
            probs = jnp.exp2(scores - top)
            total = jnp.broadcast_to(jnp.sum(probs, axis=-1, keepdims=True), wide)
            summed = jnp.dot(
                probs.astype(jnp.bfloat16), kv[rows_in, pl.ds(HEAD_DIM, HEAD_DIM)],
                preferred_element_type=jnp.float32,
            )
            top = jnp.broadcast_to(top, wide)
            if t:
                fade = jnp.exp2(tops[h] - top)
                total += sums[h] * fade
                summed += mixed[h] * fade
            tops[h] = top
            sums[h] = total
            mixed[h] = summed
            return carry

        if t:
            @pl.when(got)
            def _():
                peer_keys()
                lax.fori_loop(0, group, head, 0)
        else:
            pl.when(x > ox)(peer_keys)
            lax.fori_loop(0, group, head, 0)

    def finish_heads(ctx):
        def head(h, carry):
            cols = at(c * qh + h * HEAD_DIM, HEAD_DIM, 128)
            ctx[:, cols] = (mixed[h] / sums[h]).astype(jnp.bfloat16)
            return carry

        lax.fori_loop(0, group, head, 0)

    def share_ctx(p, ctx):
        ref = ctx.at[:, at(c * qh, qh, 128)]
        send(ref, ref, cx_send.at[8 + p], cx_recv.at[8 + p], partner)

    def ctx_ready(p, ctx):
        arrived(ctx.at[:, at(oc * qh, qh, 128)], cx_recv.at[8 + p], cx_send.at[8 + p], partner)

    def project_out(src, ctx, half, j):
        lo, width = chunks[j]
        wide = src[:, at(c * oh + lo, width, 128)].astype(jnp.float32)
        half[:, pl.ds(lo, width)] = (
            wide + jnp.dot(ctx[...], wouts[j][...], preferred_element_type=jnp.float32)
        ).astype(jnp.bfloat16)

    def heads_out(ctx, j, cc):
        return jnp.dot(
            ctx[:, at(cc * qh, qh, 128)], wouts[j][at(cc * qh, qh), :],
            preferred_element_type=jnp.float32,
        )

    def project_own(src, ctx, j):
        lo, width = chunks[j]
        wide = src[:, at(c * oh + lo, width, 128)].astype(jnp.float32)
        partial[:, pl.ds(lo, width)] = wide + heads_out(ctx, j, c)

    def project_other(ctx, half, j):
        cols = pl.ds(*chunks[j])
        half[:, cols] = (partial[:, cols] + heads_out(ctx, j, oc)).astype(jnp.bfloat16)

    n_out = len(chunks)
    own_copies = []

    def give(p, half, out, j):
        lo, width = chunks[j]
        i = 10 + p * n_out + j
        cols = at(c * oh + lo, width, 128)
        cols_in = pl.ds(lo, width)
        send(
            half.at[at(oc * rows, rows), cols_in], out.at[:, cols], cx_send.at[i], cx_recv.at[i],
            partner,
        )
        copy = pltpu.make_async_copy(
            half.at[mine, cols_in], out.at[:, cols], loc_sem.at[8 + p * n_out + j]
        )
        copy.start()
        own_copies.append(copy)

    def given(p, out, j):
        lo, width = chunks[j]
        i = 10 + p * n_out + j
        arrived(
            out.at[:, at(oc * oh + lo, width, 128)], cx_recv.at[i], cx_send.at[i], partner
        )

    def pass_on(j):
        lo, width = chunks[j]
        send(
            half1.at[:, pl.ds(lo, width)], xs2.at[:, at(c * oh + lo, width, 128)],
            ps_send.at[j], ps_recv.at[j], s_next, has_next,
        )

    def passed(j):
        lo, width = chunks[j]
        ref = xs2.at[:, at(c * oh + lo, width, 128)]
        pl.when(has_prev)(lambda: arrived(ref, ps_recv.at[j], ps_send.at[j], s_prev))
        send(ref, ref, cx_send.at[10 + 2 * n_out + j], cx_recv.at[10 + 2 * n_out + j], partner, has_prev)
        pl.when(has_prev)(
            lambda: arrived(
                xs2.at[:, at(oc * oh + lo, width, 128)], cx_recv.at[10 + 2 * n_out + j], cx_send.at[10 + 2 * n_out + j],
                partner,
            )
        )
        scale_in(xs2, lo, width, j == 0)

    for i in range(3):
        own_ready(i)
    a_start(0)
    own_ready(3)
    a_start(1)
    tables(0)
    tables(1)
    make_mask(0)
    local[6].wait()
    other_rows = at(oc * rows, rows)
    arrived(xs1.at[other_rows], cx_recv.at[6], cx_send.at[6], partner)
    scale_in(xs1, 0, oh, True)
    for i in range(4, len(pieces)):
        own_ready(i)

    def from_first():
        inc_copy.wait()
        arrived(xs2.at[other_rows], cx_recv.at[7], cx_send.at[7], partner)

    pl.when(first)(from_first)
    a_step(0, 1)
    a_step(0, 2)
    a_step(0, 3)
    b_start(0)
    a_start(2)
    b_steps(0)
    a_step(1, 1)
    gather_end(0)
    multiply(0, oh, qh, 2 * kh, True)
    finish_keys(0, kv1)
    multiply(0, oh, 0, qh, True)
    finish_queries(0)
    a_step(1, 2)
    a_step(1, 3)
    b_start(1)
    a_start(3)
    b_steps(1)
    for t in range(1, PLANES):
        kv_step(0, kv1, t)
    a_step(2, 1)
    attend(0, kv1, 0)
    attend(0, kv1, 1)
    a_step(2, 2)
    a_step(3, 1)
    attend(0, kv1, 2)
    a_step(2, 3)
    b_start(2)
    a_step(3, 2)
    attend(0, kv1, 3)
    finish_heads(ctx1)
    share_ctx(0, ctx1)
    b_start(3)
    b_steps(2)
    a_step(3, 3)
    make_mask(1)
    ctx_ready(0, ctx1)
    gather_end(1)
    project_out(xs1, ctx1, half1, 0)
    pass_on(0)
    gather_end(2)
    project_out(xs1, ctx1, half1, 1)
    pass_on(1)
    passed(0)
    multiply(*chunks[0], qh, 2 * kh, True)
    multiply(*chunks[0], 0, qh, True)
    b_steps(3)
    passed(1)
    multiply(*chunks[1], qh, 2 * kh, False)
    multiply(*chunks[1], 0, qh, False)
    gather_end(3)
    project_out(xs1, ctx1, half1, 2)
    pass_on(2)
    for j in range(n_out):
        give(0, half1, out1_ref, j)
    passed(2)
    multiply(*chunks[2], qh, 2 * kh, False)
    finish_keys(1, kv2)
    multiply(*chunks[2], 0, qh, False)
    finish_queries(1)
    kv_step(1, kv2, 1)
    attend(1, kv2, 0)
    kv_step(1, kv2, 2)
    attend(1, kv2, 1)
    kv_step(1, kv2, 3)
    attend(1, kv2, 2)
    attend(1, kv2, 3)
    finish_heads(ctx2)
    share_ctx(1, ctx2)
    for j in range(n_out):
        project_own(xs2, ctx2, j)
    ctx_ready(1, ctx2)
    for j in range(n_out):
        project_other(ctx2, half2, j)
        give(1, half2, out2_ref, j)

    for p, out in ((0, out1_ref), (1, out2_ref)):
        for j in range(n_out):
            given(p, out, j)
    for copy in own_copies:
        copy.wait()
    for copy, cond in sent:
        if cond is None:
            copy.wait_send()
        else:
            pl.when(cond)(copy.wait_send)


def per_device(
    n_section,
    activations,
    incoming,
    column_ids,
    positions,
    norm_gain,
    w_query,
    w_key,
    w_value,
    w_out,
    b_query,
    b_key,
    b_value,
):
    _, rows, d = activations.shape
    qw, kvw = w_query.shape[2], w_key.shape[2]
    qh, kh, oh = qw // CORES, kvw // CORES, d // CORES
    tok = rows * CORES
    seq_len = column_ids.shape[1]
    half = HEAD_DIM // 2
    freqs = THETA ** (-(jnp.arange(half, dtype=jnp.float32) * 2.0) / HEAD_DIM)
    signs = jnp.ones((half,), jnp.float32)
    freqs = jnp.stack([jnp.concatenate([freqs, freqs]), jnp.concatenate([-signs, signs])])
    cuts = [oh * 3 // 7, oh * 5 // 14, oh * 3 // 14]
    bf16, f32 = jnp.bfloat16, jnp.float32
    anywhere = pl.BlockSpec(memory_space=pl.ANY)
    vmem = pl.BlockSpec(memory_space=pltpu.VMEM)
    dma = pltpu.SemaphoreType.DMA
    shape = jax.ShapeDtypeStruct((rows, d), bf16)
    width = qh + 2 * kh
    jobs = 1 + len(cuts)
    z_sems = dma((jobs, PLANES - 1, 3))
    out1, out2 = pl.pallas_call(
        functools.partial(kernel, n_section, (rows, d, qw, kvw)),
        out_shape=(shape, shape),
        in_specs=[anywhere] * 6 + [vmem] * 7,
        out_specs=(anywhere, anywhere),
        scratch_shapes=[
            pltpu.VMEM((d, width), bf16),
            *[pltpu.VMEM((qw, cut), bf16) for cut in cuts],
            pltpu.VMEM((tok, d), bf16),
            pltpu.VMEM((tok, d), bf16),
            pltpu.VMEM((tok, d), bf16),
            pltpu.VMEM((tok, width), f32),
            pltpu.VMEM((tok, HEAD_DIM), f32),
            pltpu.VMEM((2, 2, tok, HEAD_DIM), f32),
            pltpu.VMEM((2, tok, HEAD_DIM), f32),
            pltpu.VMEM((HEADS // KV_HEADS, tok, HEAD_DIM), bf16),
            *[pltpu.VMEM((HEADS // KV_HEADS, tok, HEAD_DIM), f32)] * 3,
            pltpu.VMEM((seq_len, 2 * HEAD_DIM), bf16),
            pltpu.VMEM((seq_len, 2 * HEAD_DIM), bf16),
            pltpu.VMEM((tok, seq_len), f32),
            pltpu.VMEM((tok, qw), bf16),
            pltpu.VMEM((tok, qw), bf16),
            pltpu.VMEM((tok, oh), bf16),
            pltpu.VMEM((tok, oh), bf16),
            pltpu.VMEM((tok, oh), f32),
            dma((8 + 2 * len(cuts),)),
            dma((10 + 3 * len(cuts),)),
            dma((10 + 3 * len(cuts),)),
            z_sems,
            z_sems,
            z_sems,
            z_sems,
            dma((jobs, 2 * PLANES)),
            dma((jobs, 2 * PLANES)),
            dma((2, 2, PLANES)),
            dma((2, 2, PLANES)),
            dma((len(cuts),)),
            dma((len(cuts),)),
        ],
        compiler_params=pltpu.CompilerParams(
            collective_id=0, has_side_effects=True, vmem_limit_bytes=56 * 1024 * 1024
        ),
        name="two_sections",
    )(
        activations[0],
        incoming,
        w_query[0],
        w_key[0],
        w_value[0],
        w_out[0],
        norm_gain,
        b_query,
        b_key,
        b_value,
        freqs,
        column_ids,
        positions,
    )
    return (out1[None], out2[None])


def solution(mesh):
    placed = (
        P("section", "seq", None),
        P("seq", None),
        P(),
        P(),
        P("section", None),
        P("section", "seq", None),
        P("section", "seq", None),
        P("section", "seq", None),
        P("section", "seq", None),
        P("section", None),
        P("section", None),
        P("section", None),
    )
    return jax.shard_map(
        functools.partial(per_device, mesh.shape["section"]),
        mesh=mesh,
        in_specs=placed,
        out_specs=(P("section", "seq", None), P("section", "seq", None)),
        check_vma=False,
    )
```

```python
import functools
import math

import jax
import jax.numpy as jnp
import numpy as np
from jax import lax
from jax.experimental import pallas as pl
from jax.experimental.pallas import tpu as pltpu
from jax.sharding import PartitionSpec as P

HEAD_DIM = 128
HEADS = 14
KV_HEADS = 2
EPSILON = 1e-06
THETA = 1000000.0
MESH = pl.DeviceIdType.MESH

PLANES, CHIPS_X, CORES = 4, 2, 2
CHIPS = PLANES * CHIPS_X


def kernel(
    n_section,
    dims,
    x_ref,
    inc_ref,
    wq_ref,
    wk_ref,
    wv_ref,
    wo_ref,
    gain_ref,
    bq_ref,
    bk_ref,
    bv_ref,
    freq_ref,
    cols_ref,
    pos_ref,
    out1_ref,
    out2_ref,
    wkv,
    wquery,
    wout_a,
    wout_b,
    wout_c,
    xs1,
    xs2,
    hidden,
    acc,
    squares,
    turns,
    q_cols,
    qs,
    tops,
    sums,
    mixed,
    kv1,
    kv2,
    mask,
    ctx1,
    ctx2,
    half1,
    half2,
    partial,
    loc_sem,
    cx_send,
    cx_recv,
    up_send,
    up_recv,
    dn_send,
    dn_recv,
    xl_send,
    xl_recv,
    kv_send,
    kv_recv,
    ps_send,
    ps_recv,
):
    (rows, d, qw, kvw) = dims
    seq_len = rows * CHIPS * CORES
    tok = rows * CORES
    qh, kh, oh = qw // CORES, kvw // CORES, d // CORES
    group = HEADS // KV_HEADS
    wr, wor = wq_ref.shape[0], wo_ref.shape[0]

    s = lax.axis_index("section")
    me = lax.axis_index("seq")
    chip = me // CORES
    c = me % CORES
    z = chip // CHIPS_X
    x = chip % CHIPS_X
    oc = 1 - c
    ox = 1 - x

    def dev(zz, xx, cc):
        return (s, (zz * CHIPS_X + xx) * CORES + cc)

    partner = dev(z, x, oc)
    x_peer = dev(z, ox, c)
    z_up = dev(jnp.minimum(z + 1, PLANES - 1), x, c)
    z_dn = dev(jnp.maximum(z - 1, 0), x, c)

    sent = []

    def send(src, dst, ssem, rsem, target, cond=None):
        copy = pltpu.make_async_remote_copy(
            src_ref=src, dst_ref=dst, send_sem=ssem, recv_sem=rsem,
            device_id=target, device_id_type=MESH,
        )
        if cond is None:
            copy.start()
        else:
            pl.when(cond)(copy.start)
        sent.append((copy, cond))

    def arrived(ref, rsem, ssem, target):
        pltpu.make_async_remote_copy(
            src_ref=ref, dst_ref=ref, send_sem=ssem, recv_sem=rsem,
            device_id=target, device_id_type=MESH,
        ).wait_recv()

    def at(offset, size, unit=16):
        return pl.ds(pl.multiple_of(offset, unit), size)

    kv1[...] = jnp.zeros_like(kv1)
    kv2[...] = jnp.zeros_like(kv2)

    barrier = pltpu.get_barrier_semaphore()

    def greet(target):
        pl.semaphore_signal(barrier, inc=1, device_id=target, device_id_type=MESH)

    greet(partner)
    greet(x_peer)
    can_up = z < PLANES - 1
    can_dn = z > 0
    pl.when(can_up)(lambda: greet(z_up))
    pl.when(can_dn)(lambda: greet(z_dn))
    has_prev = s > 0
    has_next = s < n_section - 1
    s_prev = (jnp.maximum(s - 1, 0), me)
    s_next = (jnp.minimum(s + 1, n_section - 1), me)
    pl.when(has_prev)(lambda: greet(s_prev))
    pl.when(has_next)(lambda: greet(s_next))
    peers = 2
    for there in (can_up, can_dn, has_prev, has_next):
        peers = peers + there.astype(jnp.int32)
    pl.semaphore_wait(barrier, peers)

    row0 = chip * (CORES * wr) + c * wr
    orow0 = chip * (CORES * wr) + oc * wr
    wrow0 = chip * (CORES * wor) + c * wor
    worow0 = chip * (CORES * wor) + oc * wor
    wouts = [wout_a, wout_b, wout_c]
    chunks = []
    low = 0
    for buf in wouts:
        chunks.append((low, buf.shape[1]))
        low += buf.shape[1]
    pieces = [
        (wk_ref, wkv, row0, orow0, wr, kh, 0, 0),
        (wv_ref, wkv, row0, orow0, wr, kh, 0, kh),
        (wq_ref, wquery, row0, orow0, wr, qh, 0, 0),
    ] + [
        (wo_ref, buf, wrow0, worow0, wor, oh, lo, 0) for buf, (lo, _) in zip(wouts, chunks)
    ]
    widths = [kh, kh, qh] + [w for _, w in chunks]
    local = []
    for i, (src, dst, r0, _, n, part, lo, col) in enumerate(pieces):
        width = widths[i]
        there = dst.at[at(r0, n), pl.ds(col, width)]
        send(
            src.at[:, at(oc * part + lo, width, 128)], there, cx_send.at[i], cx_recv.at[i], partner
        )
        copy = pltpu.make_async_copy(
            src.at[:, at(c * part + lo, width, 128)], there, loc_sem.at[i]
        )
        copy.start()
        local.append(copy)

    mine = at(c * rows, rows)
    send(x_ref, xs1.at[mine], cx_send.at[6], cx_recv.at[6], partner)
    copy = pltpu.make_async_copy(x_ref, xs1.at[mine], loc_sem.at[6])
    copy.start()
    local.append(copy)
    first = s == 0
    send(inc_ref, xs2.at[mine], cx_send.at[7], cx_recv.at[7], partner, first)
    inc_copy = pltpu.make_async_copy(inc_ref, xs2.at[mine], loc_sem.at[7])
    pl.when(first)(inc_copy.start)

    def own_ready(i):
        _, dst, _, r1, n, _, _, col = pieces[i]
        local[i].wait()
        arrived(dst.at[at(r1, n), pl.ds(col, widths[i])], cx_recv.at[i], cx_send.at[i], partner)

    bufs = [wkv, wquery] + wouts
    shard = [CORES * wr] * 2 + [CORES * wor] * len(wouts)
    tails = [80] * 2 + [32] * len(wouts)

    def apart(w, zz, xx):
        return bufs[w].at[at((zz * CHIPS_X + xx) * shard[w], shard[w] - tails[w])]

    def bpart(w, zz, xx):
        return bufs[w].at[at((zz * CHIPS_X + xx + 1) * shard[w] - tails[w], tails[w])]

    def z_send(ref, w, t, part, up, cond):
        ss, rs = (up_send, up_recv) if up else (dn_send, dn_recv)
        target = z_up if up else z_dn
        send(ref, ref, ss.at[w, t, part], rs.at[w, t, part], target, cond)

    def x_send(ref, w, i, cond=None):
        send(ref, ref, xl_send.at[w, i], xl_recv.at[w, i], x_peer, cond)

    def flow(up, t):
        zz = z - t if up else z + t
        got = (z >= t) if up else (z + t <= PLANES - 1)
        on = got & (can_up if up else can_dn)
        return jnp.clip(zz, 0, PLANES - 1), got, on

    def a_start(w):
        x_send(bpart(w, z, x), w, 0)
        z_send(apart(w, z, x), w, 0, 0, True, can_up)
        z_send(apart(w, z, x), w, 0, 0, False, can_dn)
        x_send(apart(w, z, x), w, 1)

    def b_start(w):
        other = bpart(w, z, ox)
        arrived(other, xl_recv.at[w, 0], xl_send.at[w, 0], x_peer)
        for part, ref in ((1, bpart(w, z, x)), (2, other)):
            z_send(ref, w, 0, part, True, can_up)
            z_send(ref, w, 0, part, False, can_dn)

    def z_arrived(ref, w, t, part, up, got):
        ss, rs = (up_send, up_recv) if up else (dn_send, dn_recv)
        target = z_dn if up else z_up
        pl.when(got)(
            lambda: arrived(ref, rs.at[w, t - 1, part], ss.at[w, t - 1, part], target)
        )

    def a_step(w, t):
        for up in (True, False):
            zc, got, on = flow(up, t)
            ref = apart(w, zc, x)
            z_arrived(ref, w, t, 0, up, got)
            if t < PLANES - 1:
                z_send(ref, w, t, 0, up, on)
            x_send(ref, w, (1 if up else PLANES) + t, got)

    def b_step(w, t):
        for up in (True, False):
            zc, got, on = flow(up, t)
            for part, ref in ((1, bpart(w, zc, x)), (2, bpart(w, zc, ox))):
                z_arrived(ref, w, t, part, up, got)
                if t < PLANES - 1:
                    z_send(ref, w, t, part, up, on)

    def b_steps(w):
        for t in range(1, PLANES):
            b_step(w, t)

    def gather_end(w):
        arrived(apart(w, z, ox), xl_recv.at[w, 1], xl_send.at[w, 1], x_peer)
        for t in range(1, PLANES):
            for up in (True, False):
                zc, got, _ = flow(up, t)
                i = (1 if up else PLANES) + t
                pl.when(got)(
                    lambda zc=zc, i=i: arrived(
                        apart(w, zc, ox), xl_recv.at[w, i], xl_send.at[w, i], x_peer
                    )
                )

    exp_factor = HEAD_DIM ** (-0.5) * math.log2(math.e)
    micro = [s, lax.rem(s + n_section, n_section + 1)]

    def tables(p):
        own = at(chip * tok, tok, 128)
        eye = lax.broadcasted_iota(jnp.int32, (tok, tok), 0) == lax.broadcasted_iota(
            jnp.int32, (tok, tok), 1
        )

        def upright(ref):
            entries = ref[pl.ds(micro[p], 1), own].astype(jnp.float32)
            return jnp.sum(jnp.where(eye, entries, 0.0), axis=1, keepdims=True)

        q_cols[p] = jnp.broadcast_to(upright(cols_ref), (tok, HEAD_DIM))
        angles = upright(pos_ref) * freq_ref[0:1, :]
        turns[p, 0] = jnp.cos(angles)
        turns[p, 1] = jnp.sin(angles) * freq_ref[1:2, :]

    def make_mask(p):
        key_col = cols_ref[pl.ds(micro[p], 1), :].astype(jnp.float32)

        def body(i, carry):
            r = at(i * 32, 32, 32)
            q_col = q_cols[p, r, 0:1]
            shape = (32, seq_len)
            qi = chip * tok + i * 32 + lax.broadcasted_iota(jnp.int32, shape, 0)
            ki = lax.broadcasted_iota(jnp.int32, shape, 1)
            ok = (ki <= qi) & ((key_col == q_col) | (key_col == 0.0))
            mask[r, :] = jnp.where(ok, 0.0, -1e30).astype(jnp.float32)
            return carry

        lax.fori_loop(0, tok // 32, body, 0)

    def scale_in(src, lo, width, start):
        def body(i, carry):
            r = at(i * 32, 32, 32)
            total = jnp.zeros((32, 1), jnp.float32)
            for cc in range(CORES):
                cols = pl.ds(cc * oh + lo, width)
                wide = src[r, cols].astype(jnp.float32)
                hidden[r, cols] = (wide * gain_ref[:, cols]).astype(jnp.bfloat16)
                total += jnp.sum(wide * wide, axis=-1, keepdims=True)
            total = jnp.broadcast_to(total, (32, HEAD_DIM))
            squares[r, :] = total if start else squares[r, :] + total
            return carry

        lax.fori_loop(0, tok // 32, body, 0)

    def multiply(lo, width, weights, start):
        total = 0.0
        for cc in range(CORES):
            part = pl.ds(cc * oh + lo, width)
            total += jnp.dot(
                hidden[:, part], weights[part, :], preferred_element_type=jnp.float32
            )
        cols = pl.ds(0, qh) if weights is wquery else pl.ds(qh, 2 * kh)
        acc[:, cols] = total if start else acc[:, cols] + total

    def row_factor():
        return lax.rsqrt(squares[...] * (1.0 / d) + EPSILON)

    def turn(p, u):
        return u * turns[p, 0] + pltpu.roll(u, HEAD_DIM // 2, 1) * turns[p, 1]

    def kv_rows(kv, zz, xx):
        return kv.at[at((zz * CHIPS_X + xx) * tok, tok)]

    def kv_x_send(p, ref, i, cond):
        send(ref, ref, kv_send.at[p, 1, i], kv_recv.at[p, 1, i], x_peer, cond)

    def kv_z_send(p, ref, i, cond):
        send(ref, ref, kv_send.at[p, 0, i], kv_recv.at[p, 0, i], z_up, cond)

    def finish_keys(p, kv):
        factor = row_factor()
        own = at(chip * tok, tok)
        key_bias = bk_ref[:, at(c * kh, kh, 128)]
        value_bias = bv_ref[:, at(c * kh, kh, 128)]
        kv[own, pl.ds(0, kh)] = turn(p, acc[:, pl.ds(qh, kh)] * factor + key_bias).astype(
            jnp.bfloat16
        )
        kv[own, pl.ds(kh, kh)] = (acc[:, pl.ds(qh + kh, kh)] * factor + value_bias).astype(
            jnp.bfloat16
        )
        mine_kv = kv_rows(kv, z, x)
        kv_z_send(p, mine_kv, 0, can_up)
        kv_x_send(p, mine_kv, 0, x < ox)

    def finish_queries(p):
        factor = row_factor()

        def head(h, carry):
            cols = at(h * HEAD_DIM, HEAD_DIM, 128)
            query_bias = bq_ref[:, at(c * qh + h * HEAD_DIM, HEAD_DIM, 128)]
            turned = turn(p, acc[:, cols] * factor + query_bias)
            qs[h] = (turned * exp_factor).astype(jnp.bfloat16)
            return carry

        lax.fori_loop(0, group, head, 0)

    def kv_step(p, kv, t):
        zc, got, on = flow(True, t)
        ref = kv_rows(kv, zc, x)
        pl.when(got)(
            lambda: arrived(ref, kv_recv.at[p, 0, t - 1], kv_send.at[p, 0, t - 1], z_dn)
        )
        if t < PLANES - 1:
            kv_z_send(p, ref, t, on)
        kv_x_send(p, ref, t, got)

    plane = CHIPS_X * tok

    def attend(p, kv, t):
        zc, got, _ = flow(True, t)
        peer_keys = lambda: arrived(
            kv_rows(kv, zc, ox), kv_recv.at[p, 1, t], kv_send.at[p, 1, t], x_peer
        )

        def head(h, carry):
            rows_in = at(zc * plane, plane, 128)
            scores = lax.dot_general(
                qs[h], kv[rows_in, pl.ds(0, HEAD_DIM)], (((1,), (1,)), ((), ())),
                preferred_element_type=jnp.float32,
            )
            scores = scores + mask[:, rows_in]
            top = jnp.max(scores, axis=-1, keepdims=True)
            wide = (tok, HEAD_DIM)
            if t:
                top = jnp.maximum(top, tops[h, :, 0:1])
            probs = jnp.exp2(scores - top)
            total = jnp.broadcast_to(jnp.sum(probs, axis=-1, keepdims=True), wide)
            summed = jnp.dot(
                probs.astype(jnp.bfloat16), kv[rows_in, pl.ds(HEAD_DIM, HEAD_DIM)],
                preferred_element_type=jnp.float32,
            )
            top = jnp.broadcast_to(top, wide)
            if t:
                fade = jnp.exp2(tops[h] - top)
                total += sums[h] * fade
                summed += mixed[h] * fade
            tops[h] = top
            sums[h] = total
            mixed[h] = summed
            return carry

        if t:
            @pl.when(got)
            def _():
                peer_keys()
                lax.fori_loop(0, group, head, 0)
        else:
            pl.when(x > ox)(peer_keys)
            lax.fori_loop(0, group, head, 0)

    def finish_heads(ctx):
        def head(h, carry):
            cols = at(c * qh + h * HEAD_DIM, HEAD_DIM, 128)
            ctx[:, cols] = (mixed[h] / sums[h]).astype(jnp.bfloat16)
            return carry

        lax.fori_loop(0, group, head, 0)

    def share_ctx(p, ctx):
        ref = ctx.at[:, at(c * qh, qh, 128)]
        send(ref, ref, cx_send.at[8 + p], cx_recv.at[8 + p], partner)

    def ctx_ready(p, ctx):
        arrived(ctx.at[:, at(oc * qh, qh, 128)], cx_recv.at[8 + p], cx_send.at[8 + p], partner)

    def project_out(src, ctx, half, j):
        lo, width = chunks[j]
        wide = src[:, at(c * oh + lo, width, 128)].astype(jnp.float32)
        half[:, pl.ds(lo, width)] = (
            wide + jnp.dot(ctx[...], wouts[j][...], preferred_element_type=jnp.float32)
        ).astype(jnp.bfloat16)

    def heads_out(ctx, j, cc):
        return jnp.dot(
            ctx[:, at(cc * qh, qh, 128)], wouts[j][at(cc * qh, qh), :],
            preferred_element_type=jnp.float32,
        )

    def project_own(src, ctx, j):
        lo, width = chunks[j]
        wide = src[:, at(c * oh + lo, width, 128)].astype(jnp.float32)
        partial[:, pl.ds(lo, width)] = wide + heads_out(ctx, j, c)

    def project_other(ctx, half, j):
        cols = pl.ds(*chunks[j])
        half[:, cols] = (partial[:, cols] + heads_out(ctx, j, oc)).astype(jnp.bfloat16)

    n_out = len(chunks)
    own_copies = []

    def give(p, half, out, j):
        lo, width = chunks[j]
        i = 10 + p * n_out + j
        cols = at(c * oh + lo, width, 128)
        cols_in = pl.ds(lo, width)
        send(
            half.at[at(oc * rows, rows), cols_in], out.at[:, cols], cx_send.at[i], cx_recv.at[i],
            partner,
        )
        copy = pltpu.make_async_copy(
            half.at[mine, cols_in], out.at[:, cols], loc_sem.at[8 + p * n_out + j]
        )
        copy.start()
        own_copies.append(copy)

    def given(p, out, j):
        lo, width = chunks[j]
        i = 10 + p * n_out + j
        arrived(
            out.at[:, at(oc * oh + lo, width, 128)], cx_recv.at[i], cx_send.at[i], partner
        )

    def pass_on(j):
        lo, width = chunks[j]
        send(
            half1.at[:, pl.ds(lo, width)], xs2.at[:, at(c * oh + lo, width, 128)],
            ps_send.at[j], ps_recv.at[j], s_next, has_next,
        )

    def passed(j):
        lo, width = chunks[j]
        ref = xs2.at[:, at(c * oh + lo, width, 128)]
        pl.when(has_prev)(lambda: arrived(ref, ps_recv.at[j], ps_send.at[j], s_prev))
        send(ref, ref, cx_send.at[10 + 2 * n_out + j], cx_recv.at[10 + 2 * n_out + j], partner, has_prev)
        pl.when(has_prev)(
            lambda: arrived(
                xs2.at[:, at(oc * oh + lo, width, 128)], cx_recv.at[10 + 2 * n_out + j], cx_send.at[10 + 2 * n_out + j],
                partner,
            )
        )
        scale_in(xs2, lo, width, j == 0)

    for i in range(2):
        own_ready(i)
    a_start(0)
    own_ready(2)
    a_start(1)
    tables(0)
    local[6].wait()
    other_rows = at(oc * rows, rows)
    arrived(xs1.at[other_rows], cx_recv.at[6], cx_send.at[6], partner)
    scale_in(xs1, 0, oh, True)
    a_step(0, 1)
    make_mask(0)
    a_step(0, 2)
    tables(1)
    a_step(0, 3)
    b_start(0)
    b_steps(0)
    for i in range(3, len(pieces)):
        own_ready(i)

    def from_first():
        inc_copy.wait()
        arrived(xs2.at[other_rows], cx_recv.at[7], cx_send.at[7], partner)

    pl.when(first)(from_first)
    a_step(1, 1)
    gather_end(0)
    multiply(0, oh, wkv, True)
    finish_keys(0, kv1)
    a_step(1, 2)
    a_start(2)
    kv_step(0, kv1, 1)
    a_step(1, 3)
    kv_step(0, kv1, 2)
    b_start(1)
    b_steps(1)
    kv_step(0, kv1, 3)
    a_step(2, 1)
    a_start(3)
    gather_end(1)
    multiply(0, oh, wquery, True)
    finish_queries(0)
    a_step(2, 2)
    attend(0, kv1, 0)
    attend(0, kv1, 1)
    a_step(2, 3)
    b_start(2)
    attend(0, kv1, 2)
    b_step(2, 1)
    attend(0, kv1, 3)
    finish_heads(ctx1)
    share_ctx(0, ctx1)
    b_step(2, 2)
    b_step(2, 3)
    a_step(3, 1)
    a_start(4)
    ctx_ready(0, ctx1)
    gather_end(2)
    project_out(xs1, ctx1, half1, 0)
    pass_on(0)
    a_step(3, 2)
    make_mask(1)
    a_step(3, 3)
    b_start(3)
    a_step(4, 1)
    b_step(3, 1)
    a_step(4, 2)
    b_step(3, 2)
    b_step(3, 3)
    a_step(4, 3)
    b_start(4)
    gather_end(3)
    project_out(xs1, ctx1, half1, 1)
    pass_on(1)
    b_steps(4)
    passed(0)
    multiply(*chunks[0], wkv, True)
    multiply(*chunks[0], wquery, True)
    gather_end(4)
    project_out(xs1, ctx1, half1, 2)
    pass_on(2)
    for j in range(n_out):
        give(0, half1, out1_ref, j)
    passed(1)
    multiply(*chunks[1], wkv, False)
    multiply(*chunks[1], wquery, False)
    passed(2)
    multiply(*chunks[2], wkv, False)
    finish_keys(1, kv2)
    multiply(*chunks[2], wquery, False)
    finish_queries(1)
    kv_step(1, kv2, 1)
    attend(1, kv2, 0)
    kv_step(1, kv2, 2)
    attend(1, kv2, 1)
    kv_step(1, kv2, 3)
    attend(1, kv2, 2)
    attend(1, kv2, 3)
    finish_heads(ctx2)
    share_ctx(1, ctx2)
    for j in range(n_out):
        project_own(xs2, ctx2, j)
    ctx_ready(1, ctx2)
    for j in range(n_out):
        project_other(ctx2, half2, j)
        give(1, half2, out2_ref, j)

    for p, out in ((0, out1_ref), (1, out2_ref)):
        for j in range(n_out):
            given(p, out, j)
    for copy in own_copies:
        copy.wait()
    for copy, cond in sent:
        if cond is None:
            copy.wait_send()
        else:
            pl.when(cond)(copy.wait_send)


def per_device(
    n_section,
    activations,
    incoming,
    column_ids,
    positions,
    norm_gain,
    w_query,
    w_key,
    w_value,
    w_out,
    b_query,
    b_key,
    b_value,
):
    _, rows, d = activations.shape
    qw, kvw = w_query.shape[2], w_key.shape[2]
    qh, kh, oh = qw // CORES, kvw // CORES, d // CORES
    tok = rows * CORES
    seq_len = column_ids.shape[1]
    half = HEAD_DIM // 2
    freqs = THETA ** (-(np.arange(half) * 2.0) / HEAD_DIM)
    signs = np.ones((half,))
    freqs = np.stack([np.concatenate([freqs, freqs]), np.concatenate([-signs, signs])])
    freqs = freqs.astype(np.float32)
    cuts = [oh * 3 // 7, oh * 3 // 7, oh // 7]
    bf16, f32 = jnp.bfloat16, jnp.float32
    anywhere = pl.BlockSpec(memory_space=pl.ANY)
    vmem = pl.BlockSpec(memory_space=pltpu.VMEM)
    dma = pltpu.SemaphoreType.DMA
    shape = jax.ShapeDtypeStruct((rows, d), bf16)
    width = qh + 2 * kh
    jobs = 2 + len(cuts)
    z_sems = dma((jobs, PLANES - 1, 3))
    out1, out2 = pl.pallas_call(
        functools.partial(kernel, n_section, (rows, d, qw, kvw)),
        out_shape=(shape, shape),
        in_specs=[anywhere] * 6 + [vmem] * 7,
        out_specs=(anywhere, anywhere),
        scratch_shapes=[
            pltpu.VMEM((d, 2 * kh), bf16),
            pltpu.VMEM((d, qh), bf16),
            *[pltpu.VMEM((qw, cut), bf16) for cut in cuts],
            pltpu.VMEM((tok, d), bf16),
            pltpu.VMEM((tok, d), bf16),
            pltpu.VMEM((tok, d), bf16),
            pltpu.VMEM((tok, width), f32),
            pltpu.VMEM((tok, HEAD_DIM), f32),
            pltpu.VMEM((2, 2, tok, HEAD_DIM), f32),
            pltpu.VMEM((2, tok, HEAD_DIM), f32),
            pltpu.VMEM((HEADS // KV_HEADS, tok, HEAD_DIM), bf16),
            *[pltpu.VMEM((HEADS // KV_HEADS, tok, HEAD_DIM), f32)] * 3,
            pltpu.VMEM((seq_len, 2 * HEAD_DIM), bf16),
            pltpu.VMEM((seq_len, 2 * HEAD_DIM), bf16),
            pltpu.VMEM((tok, seq_len), f32),
            pltpu.VMEM((tok, qw), bf16),
            pltpu.VMEM((tok, qw), bf16),
            pltpu.VMEM((tok, oh), bf16),
            pltpu.VMEM((tok, oh), bf16),
            pltpu.VMEM((tok, oh), f32),
            dma((8 + 2 * len(cuts),)),
            dma((10 + 3 * len(cuts),)),
            dma((10 + 3 * len(cuts),)),
            z_sems,
            z_sems,
            z_sems,
            z_sems,
            dma((jobs, 2 * PLANES)),
            dma((jobs, 2 * PLANES)),
            dma((2, 2, PLANES)),
            dma((2, 2, PLANES)),
            dma((len(cuts),)),
            dma((len(cuts),)),
        ],
        compiler_params=pltpu.CompilerParams(
            collective_id=0, has_side_effects=True, vmem_limit_bytes=56 * 1024 * 1024
        ),
        name="two_sections",
    )(
        activations[0],
        incoming,
        w_query[0],
        w_key[0],
        w_value[0],
        w_out[0],
        norm_gain,
        b_query,
        b_key,
        b_value,
        freqs,
        column_ids,
        positions,
    )
    return (out1[None], out2[None])


def solution(mesh):
    placed = (
        P("section", "seq", None),
        P("seq", None),
        P(),
        P(),
        P("section", None),
        P("section", "seq", None),
        P("section", "seq", None),
        P("section", "seq", None),
        P("section", "seq", None),
        P("section", None),
        P("section", None),
        P("section", None),
    )
    return jax.shard_map(
        functools.partial(per_device, mesh.shape["section"]),
        mesh=mesh,
        in_specs=placed,
        out_specs=(P("section", "seq", None), P("section", "seq", None)),
        check_vma=False,
    )
```

```python
import functools
import math

import jax
import jax.numpy as jnp
import numpy as np
from jax import lax
from jax.experimental import pallas as pl
from jax.experimental.pallas import tpu as pltpu
from jax.sharding import PartitionSpec as P

HEAD_DIM = 128
HEADS = 14
KV_HEADS = 2
EPSILON = 1e-06
THETA = 1000000.0
MESH = pl.DeviceIdType.MESH

PLANES, CHIPS_X, CORES = 4, 2, 2
CHIPS = PLANES * CHIPS_X


def kernel(
    n_section,
    dims,
    x_ref,
    inc_ref,
    wq_ref,
    wk_ref,
    wv_ref,
    wo_ref,
    gain_ref,
    bq_ref,
    bk_ref,
    bv_ref,
    freq_ref,
    cols_ref,
    pos_ref,
    out1_ref,
    out2_ref,
    wkv,
    wquery,
    wout_a,
    wout_b,
    wout_c,
    xs1,
    xs2,
    hidden,
    acc,
    squares,
    turns,
    q_cols,
    qs,
    tops,
    sums,
    mixed,
    kv1,
    kv2,
    mask,
    ctx1,
    ctx2,
    half1,
    half2,
    partial,
    loc_sem,
    cx_send,
    cx_recv,
    up_send,
    up_recv,
    dn_send,
    dn_recv,
    xl_send,
    xl_recv,
    kv_send,
    kv_recv,
    ps_send,
    ps_recv,
):
    (rows, d, qw, kvw) = dims
    seq_len = rows * CHIPS * CORES
    tok = rows * CORES
    qh, kh, oh = qw // CORES, kvw // CORES, d // CORES
    group = HEADS // KV_HEADS
    wr, wor = wq_ref.shape[0], wo_ref.shape[0]

    s = lax.axis_index("section")
    me = lax.axis_index("seq")
    chip = me // CORES
    c = me % CORES
    z = chip // CHIPS_X
    x = chip % CHIPS_X
    oc = 1 - c
    ox = 1 - x

    def dev(zz, xx, cc):
        return (s, (zz * CHIPS_X + xx) * CORES + cc)

    partner = dev(z, x, oc)
    x_peer = dev(z, ox, c)
    z_up = dev(jnp.minimum(z + 1, PLANES - 1), x, c)
    z_dn = dev(jnp.maximum(z - 1, 0), x, c)

    sent = []

    def send(src, dst, ssem, rsem, target, cond=None):
        copy = pltpu.make_async_remote_copy(
            src_ref=src, dst_ref=dst, send_sem=ssem, recv_sem=rsem,
            device_id=target, device_id_type=MESH,
        )
        if cond is None:
            copy.start()
        else:
            pl.when(cond)(copy.start)
        sent.append((copy, cond))

    def arrived(ref, rsem, ssem, target):
        pltpu.make_async_remote_copy(
            src_ref=ref, dst_ref=ref, send_sem=ssem, recv_sem=rsem,
            device_id=target, device_id_type=MESH,
        ).wait_recv()

    def at(offset, size, unit=16):
        return pl.ds(pl.multiple_of(offset, unit), size)

    kv1[...] = jnp.zeros_like(kv1)
    kv2[...] = jnp.zeros_like(kv2)

    barrier = pltpu.get_barrier_semaphore()

    def greet(target):
        pl.semaphore_signal(barrier, inc=1, device_id=target, device_id_type=MESH)

    greet(partner)
    greet(x_peer)
    can_up = z < PLANES - 1
    can_dn = z > 0
    pl.when(can_up)(lambda: greet(z_up))
    pl.when(can_dn)(lambda: greet(z_dn))
    has_prev = s > 0
    has_next = s < n_section - 1
    s_prev = (jnp.maximum(s - 1, 0), me)
    s_next = (jnp.minimum(s + 1, n_section - 1), me)
    pl.when(has_prev)(lambda: greet(s_prev))
    pl.when(has_next)(lambda: greet(s_next))
    peers = 2
    for there in (can_up, can_dn, has_prev, has_next):
        peers = peers + there.astype(jnp.int32)
    pl.semaphore_wait(barrier, peers)

    row0 = chip * (CORES * wr) + c * wr
    orow0 = chip * (CORES * wr) + oc * wr
    wrow0 = chip * (CORES * wor) + c * wor
    worow0 = chip * (CORES * wor) + oc * wor
    wouts = [wout_a, wout_b, wout_c]
    chunks = []
    low = 0
    for buf in wouts:
        chunks.append((low, buf.shape[1]))
        low += buf.shape[1]
    pieces = [
        (wk_ref, wkv, row0, orow0, wr, kh, 0, 0),
        (wv_ref, wkv, row0, orow0, wr, kh, 0, kh),
        (wq_ref, wquery, row0, orow0, wr, qh, 0, 0),
    ] + [
        (wo_ref, buf, wrow0, worow0, wor, oh, lo, 0) for buf, (lo, _) in zip(wouts, chunks)
    ]
    widths = [kh, kh, qh] + [w for _, w in chunks]
    local = []
    for i, (src, dst, r0, _, n, part, lo, col) in enumerate(pieces):
        width = widths[i]
        there = dst.at[at(r0, n), pl.ds(col, width)]
        send(
            src.at[:, at(oc * part + lo, width, 128)], there, cx_send.at[i], cx_recv.at[i], partner
        )
        copy = pltpu.make_async_copy(
            src.at[:, at(c * part + lo, width, 128)], there, loc_sem.at[i]
        )
        copy.start()
        local.append(copy)

    mine = at(c * rows, rows)
    send(x_ref, xs1.at[mine], cx_send.at[6], cx_recv.at[6], partner)
    copy = pltpu.make_async_copy(x_ref, xs1.at[mine], loc_sem.at[6])
    copy.start()
    local.append(copy)
    first = s == 0
    send(inc_ref, xs2.at[mine], cx_send.at[7], cx_recv.at[7], partner, first)
    inc_copy = pltpu.make_async_copy(inc_ref, xs2.at[mine], loc_sem.at[7])
    pl.when(first)(inc_copy.start)

    def own_ready(i):
        _, dst, _, r1, n, _, _, col = pieces[i]
        local[i].wait()
        arrived(dst.at[at(r1, n), pl.ds(col, widths[i])], cx_recv.at[i], cx_send.at[i], partner)

    bufs = [wkv, wquery] + wouts
    shard = [CORES * wr] * 2 + [CORES * wor] * len(wouts)
    tails = [80] * 2 + [32] * len(wouts)

    def apart(w, zz, xx):
        return bufs[w].at[at((zz * CHIPS_X + xx) * shard[w], shard[w] - tails[w])]

    def bpart(w, zz, xx):
        return bufs[w].at[at((zz * CHIPS_X + xx + 1) * shard[w] - tails[w], tails[w])]

    def z_send(ref, w, t, part, up, cond):
        ss, rs = (up_send, up_recv) if up else (dn_send, dn_recv)
        target = z_up if up else z_dn
        send(ref, ref, ss.at[w, t, part], rs.at[w, t, part], target, cond)

    def x_send(ref, w, i, cond=None):
        send(ref, ref, xl_send.at[w, i], xl_recv.at[w, i], x_peer, cond)

    def flow(up, t):
        zz = z - t if up else z + t
        got = (z >= t) if up else (z + t <= PLANES - 1)
        on = got & (can_up if up else can_dn)
        return jnp.clip(zz, 0, PLANES - 1), got, on

    def a_start(w):
        x_send(bpart(w, z, x), w, 0)
        z_send(apart(w, z, x), w, 0, 0, True, can_up)
        z_send(apart(w, z, x), w, 0, 0, False, can_dn)
        x_send(apart(w, z, x), w, 1)

    def b_start(w):
        other = bpart(w, z, ox)
        arrived(other, xl_recv.at[w, 0], xl_send.at[w, 0], x_peer)
        for part, ref in ((1, bpart(w, z, x)), (2, other)):
            z_send(ref, w, 0, part, True, can_up)
            z_send(ref, w, 0, part, False, can_dn)

    def z_arrived(ref, w, t, part, up, got):
        ss, rs = (up_send, up_recv) if up else (dn_send, dn_recv)
        target = z_dn if up else z_up
        pl.when(got)(
            lambda: arrived(ref, rs.at[w, t - 1, part], ss.at[w, t - 1, part], target)
        )

    def a_step(w, t):
        for up in (True, False):
            zc, got, on = flow(up, t)
            ref = apart(w, zc, x)
            z_arrived(ref, w, t, 0, up, got)
            if t < PLANES - 1:
                z_send(ref, w, t, 0, up, on)
            x_send(ref, w, (1 if up else PLANES) + t, got)

    def b_step(w, t):
        for up in (True, False):
            zc, got, on = flow(up, t)
            for part, ref in ((1, bpart(w, zc, x)), (2, bpart(w, zc, ox))):
                z_arrived(ref, w, t, part, up, got)
                if t < PLANES - 1:
                    z_send(ref, w, t, part, up, on)

    def step(w, t):
        a_step(w, t)
        b_step(w, t)

    def gather_end(w):
        arrived(apart(w, z, ox), xl_recv.at[w, 1], xl_send.at[w, 1], x_peer)
        for t in range(1, PLANES):
            for up in (True, False):
                zc, got, _ = flow(up, t)
                i = (1 if up else PLANES) + t
                pl.when(got)(
                    lambda zc=zc, i=i: arrived(
                        apart(w, zc, ox), xl_recv.at[w, i], xl_send.at[w, i], x_peer
                    )
                )

    exp_factor = HEAD_DIM ** (-0.5) * math.log2(math.e)
    micro = [s, lax.rem(s + n_section, n_section + 1)]

    def tables(p):
        own = at(chip * tok, tok, 128)
        eye = lax.broadcasted_iota(jnp.int32, (tok, tok), 0) == lax.broadcasted_iota(
            jnp.int32, (tok, tok), 1
        )

        def upright(ref):
            entries = ref[pl.ds(micro[p], 1), own].astype(jnp.float32)
            return jnp.sum(jnp.where(eye, entries, 0.0), axis=1, keepdims=True)

        q_cols[p] = jnp.broadcast_to(upright(cols_ref), (tok, HEAD_DIM))
        angles = upright(pos_ref) * freq_ref[0:1, :]
        turns[p, 0] = jnp.cos(angles)
        turns[p, 1] = jnp.sin(angles) * freq_ref[1:2, :]

    def make_mask(p):
        key_col = cols_ref[pl.ds(micro[p], 1), :].astype(jnp.float32)

        def body(i, carry):
            r = at(i * 32, 32, 32)
            q_col = q_cols[p, r, 0:1]
            shape = (32, seq_len)
            qi = chip * tok + i * 32 + lax.broadcasted_iota(jnp.int32, shape, 0)
            ki = lax.broadcasted_iota(jnp.int32, shape, 1)
            ok = (ki <= qi) & ((key_col == q_col) | (key_col == 0.0))
            mask[r, :] = jnp.where(ok, 0.0, -1e30).astype(jnp.float32)
            return carry

        lax.fori_loop(0, tok // 32, body, 0)

    def scale_in(src, lo, width, start):
        def body(i, carry):
            r = at(i * 32, 32, 32)
            total = jnp.zeros((32, 1), jnp.float32)
            for cc in range(CORES):
                cols = pl.ds(cc * oh + lo, width)
                wide = src[r, cols].astype(jnp.float32)
                hidden[r, cols] = (wide * gain_ref[:, cols]).astype(jnp.bfloat16)
                total += jnp.sum(wide * wide, axis=-1, keepdims=True)
            total = jnp.broadcast_to(total, (32, HEAD_DIM))
            squares[r, :] = total if start else squares[r, :] + total
            return carry

        lax.fori_loop(0, tok // 32, body, 0)

    def multiply(lo, width, weights, start):
        total = 0.0
        for cc in range(CORES):
            part = pl.ds(cc * oh + lo, width)
            total += jnp.dot(
                hidden[:, part], weights[part, :], preferred_element_type=jnp.float32
            )
        cols = pl.ds(0, qh) if weights is wquery else pl.ds(qh, 2 * kh)
        acc[:, cols] = total if start else acc[:, cols] + total

    def row_factor():
        return lax.rsqrt(squares[...] * (1.0 / d) + EPSILON)

    def turn(p, u):
        return u * turns[p, 0] + pltpu.roll(u, HEAD_DIM // 2, 1) * turns[p, 1]

    def kv_rows(kv, zz, xx):
        return kv.at[at((zz * CHIPS_X + xx) * tok, tok)]

    def kv_x_send(p, ref, i, cond):
        send(ref, ref, kv_send.at[p, 1, i], kv_recv.at[p, 1, i], x_peer, cond)

    def kv_z_send(p, ref, i, cond):
        send(ref, ref, kv_send.at[p, 0, i], kv_recv.at[p, 0, i], z_up, cond)

    def finish_keys(p, kv):
        factor = row_factor()
        own = at(chip * tok, tok)
        key_bias = bk_ref[:, at(c * kh, kh, 128)]
        value_bias = bv_ref[:, at(c * kh, kh, 128)]
        kv[own, pl.ds(0, kh)] = turn(p, acc[:, pl.ds(qh, kh)] * factor + key_bias).astype(
            jnp.bfloat16
        )
        kv[own, pl.ds(kh, kh)] = (acc[:, pl.ds(qh + kh, kh)] * factor + value_bias).astype(
            jnp.bfloat16
        )
        mine_kv = kv_rows(kv, z, x)
        kv_z_send(p, mine_kv, 0, can_up)
        kv_x_send(p, mine_kv, 0, x < ox)

    def finish_queries(p):
        factor = row_factor()

        def head(h):
            cols = pl.ds(h * HEAD_DIM, HEAD_DIM)
            query_bias = bq_ref[:, at(c * qh + h * HEAD_DIM, HEAD_DIM, 128)]
            turned = turn(p, acc[:, cols] * factor + query_bias)
            qs[h] = (turned * exp_factor).astype(jnp.bfloat16)

        for h in range(group):
            head(h)

    def kv_step(p, kv, t):
        zc, got, on = flow(True, t)
        ref = kv_rows(kv, zc, x)
        pl.when(got)(
            lambda: arrived(ref, kv_recv.at[p, 0, t - 1], kv_send.at[p, 0, t - 1], z_dn)
        )
        if t < PLANES - 1:
            kv_z_send(p, ref, t, on)
        kv_x_send(p, ref, t, got)

    plane = CHIPS_X * tok

    def attend(p, kv, t):
        zc, got, _ = flow(True, t)
        peer_keys = lambda: arrived(
            kv_rows(kv, zc, ox), kv_recv.at[p, 1, t], kv_send.at[p, 1, t], x_peer
        )

        def heads():
            rows_in = at(zc * plane, plane, 128)
            all_rows = (group * tok, HEAD_DIM)
            wide = (group, tok, HEAD_DIM)
            scores = lax.dot_general(
                qs[...].reshape(all_rows), kv[rows_in, pl.ds(0, HEAD_DIM)],
                (((1,), (1,)), ((), ())), preferred_element_type=jnp.float32,
            )
            scores = scores.reshape(group, tok, plane) + mask[:, rows_in][None]
            top = jnp.max(scores, axis=-1, keepdims=True)
            if t:
                top = jnp.maximum(top, tops[:, :, 0:1])
            probs = jnp.exp2(scores - top)
            total = jnp.broadcast_to(jnp.sum(probs, axis=-1, keepdims=True), wide)
            summed = jnp.dot(
                probs.astype(jnp.bfloat16).reshape(group * tok, plane),
                kv[rows_in, pl.ds(HEAD_DIM, HEAD_DIM)], preferred_element_type=jnp.float32,
            ).reshape(wide)
            top = jnp.broadcast_to(top, wide)
            if t:
                fade = jnp.exp2(tops[...] - top)
                total += sums[...] * fade
                summed += mixed[...] * fade
            tops[...] = top
            sums[...] = total
            mixed[...] = summed

        if t:
            @pl.when(got)
            def _():
                peer_keys()
                heads()
        else:
            pl.when(x > ox)(peer_keys)
            heads()

    def finish_heads(ctx):
        def head(h):
            cols = at(c * qh + h * HEAD_DIM, HEAD_DIM, 128)
            ctx[:, cols] = (mixed[h] / sums[h]).astype(jnp.bfloat16)

        for h in range(group):
            head(h)

    def share_ctx(p, ctx):
        ref = ctx.at[:, at(c * qh, qh, 128)]
        send(ref, ref, cx_send.at[8 + p], cx_recv.at[8 + p], partner)

    def ctx_ready(p, ctx):
        arrived(ctx.at[:, at(oc * qh, qh, 128)], cx_recv.at[8 + p], cx_send.at[8 + p], partner)

    def project_out(src, ctx, half, j):
        lo, width = chunks[j]
        wide = src[:, at(c * oh + lo, width, 128)].astype(jnp.float32)
        half[:, pl.ds(lo, width)] = (
            wide + jnp.dot(ctx[...], wouts[j][...], preferred_element_type=jnp.float32)
        ).astype(jnp.bfloat16)

    def heads_out(ctx, j, cc):
        return jnp.dot(
            ctx[:, at(cc * qh, qh, 128)], wouts[j][at(cc * qh, qh), :],
            preferred_element_type=jnp.float32,
        )

    def project_own(src, ctx, j):
        lo, width = chunks[j]
        wide = src[:, at(c * oh + lo, width, 128)].astype(jnp.float32)
        partial[:, pl.ds(lo, width)] = wide + heads_out(ctx, j, c)

    def project_other(ctx, half, j):
        cols = pl.ds(*chunks[j])
        half[:, cols] = (partial[:, cols] + heads_out(ctx, j, oc)).astype(jnp.bfloat16)

    n_out = len(chunks)
    own_copies = []

    def give(p, half, out, j):
        lo, width = chunks[j]
        i = 10 + p * n_out + j
        cols = at(c * oh + lo, width, 128)
        cols_in = pl.ds(lo, width)
        send(
            half.at[at(oc * rows, rows), cols_in], out.at[:, cols], cx_send.at[i], cx_recv.at[i],
            partner,
        )
        copy = pltpu.make_async_copy(
            half.at[mine, cols_in], out.at[:, cols], loc_sem.at[8 + p * n_out + j]
        )
        copy.start()
        own_copies.append(copy)

    def given(p, out, j):
        lo, width = chunks[j]
        i = 10 + p * n_out + j
        arrived(
            out.at[:, at(oc * oh + lo, width, 128)], cx_recv.at[i], cx_send.at[i], partner
        )

    def pass_on(j):
        lo, width = chunks[j]
        send(
            half1.at[:, pl.ds(lo, width)], xs2.at[:, at(c * oh + lo, width, 128)],
            ps_send.at[j], ps_recv.at[j], s_next, has_next,
        )

    def passed(j):
        lo, width = chunks[j]
        ref = xs2.at[:, at(c * oh + lo, width, 128)]
        pl.when(has_prev)(lambda: arrived(ref, ps_recv.at[j], ps_send.at[j], s_prev))
        send(ref, ref, cx_send.at[10 + 2 * n_out + j], cx_recv.at[10 + 2 * n_out + j], partner, has_prev)
        pl.when(has_prev)(
            lambda: arrived(
                xs2.at[:, at(oc * oh + lo, width, 128)], cx_recv.at[10 + 2 * n_out + j], cx_send.at[10 + 2 * n_out + j],
                partner,
            )
        )
        scale_in(xs2, lo, width, j == 0)

    for i in range(2):
        own_ready(i)
    a_start(0)
    own_ready(2)
    a_start(1)
    tables(0)
    local[6].wait()
    other_rows = at(oc * rows, rows)
    arrived(xs1.at[other_rows], cx_recv.at[6], cx_send.at[6], partner)
    scale_in(xs1, 0, oh, True)
    b_start(0)
    step(0, 1)
    make_mask(0)
    step(0, 2)
    tables(1)
    for i in range(3, len(pieces)):
        own_ready(i)

    def from_first():
        inc_copy.wait()
        arrived(xs2.at[other_rows], cx_recv.at[7], cx_send.at[7], partner)

    pl.when(first)(from_first)
    step(0, 3)
    b_start(1)
    gather_end(0)
    multiply(0, oh, wkv, True)
    finish_keys(0, kv1)
    step(1, 1)
    a_start(2)
    kv_step(0, kv1, 1)
    step(1, 2)
    kv_step(0, kv1, 2)
    b_start(2)
    step(1, 3)
    kv_step(0, kv1, 3)
    a_start(3)
    step(2, 1)
    gather_end(1)
    multiply(0, oh, wquery, True)
    finish_queries(0)
    step(2, 2)
    attend(0, kv1, 0)
    b_start(3)
    attend(0, kv1, 1)
    step(2, 3)
    a_start(4)
    attend(0, kv1, 2)
    step(3, 1)
    attend(0, kv1, 3)
    finish_heads(ctx1)
    share_ctx(0, ctx1)
    b_start(4)
    step(3, 2)
    ctx_ready(0, ctx1)
    gather_end(2)
    project_out(xs1, ctx1, half1, 0)
    pass_on(0)
    step(4, 1)
    step(3, 3)
    make_mask(1)
    step(4, 2)
    gather_end(3)
    project_out(xs1, ctx1, half1, 1)
    pass_on(1)
    step(4, 3)
    passed(0)
    multiply(*chunks[0], wkv, True)
    multiply(*chunks[0], wquery, True)
    gather_end(4)
    project_out(xs1, ctx1, half1, 2)
    pass_on(2)
    for j in range(n_out):
        give(0, half1, out1_ref, j)
    passed(1)
    multiply(*chunks[1], wkv, False)
    multiply(*chunks[1], wquery, False)
    passed(2)
    multiply(*chunks[2], wkv, False)
    finish_keys(1, kv2)
    multiply(*chunks[2], wquery, False)
    finish_queries(1)
    kv_step(1, kv2, 1)
    attend(1, kv2, 0)
    kv_step(1, kv2, 2)
    attend(1, kv2, 1)
    kv_step(1, kv2, 3)
    attend(1, kv2, 2)
    attend(1, kv2, 3)
    finish_heads(ctx2)
    share_ctx(1, ctx2)
    for j in range(n_out):
        project_own(xs2, ctx2, j)
    ctx_ready(1, ctx2)
    for j in range(n_out):
        project_other(ctx2, half2, j)
        give(1, half2, out2_ref, j)

    for p, out in ((0, out1_ref), (1, out2_ref)):
        for j in range(n_out):
            given(p, out, j)
    for copy in own_copies:
        copy.wait()
    for copy, cond in sent:
        if cond is None:
            copy.wait_send()
        else:
            pl.when(cond)(copy.wait_send)


def per_device(
    n_section,
    activations,
    incoming,
    column_ids,
    positions,
    norm_gain,
    w_query,
    w_key,
    w_value,
    w_out,
    b_query,
    b_key,
    b_value,
):
    _, rows, d = activations.shape
    qw, kvw = w_query.shape[2], w_key.shape[2]
    qh, kh, oh = qw // CORES, kvw // CORES, d // CORES
    tok = rows * CORES
    seq_len = column_ids.shape[1]
    half = HEAD_DIM // 2
    freqs = THETA ** (-(np.arange(half) * 2.0) / HEAD_DIM)
    signs = np.ones((half,))
    freqs = np.stack([np.concatenate([freqs, freqs]), np.concatenate([-signs, signs])])
    freqs = freqs.astype(np.float32)
    cuts = [oh * 3 // 7, oh * 5 // 14, oh * 3 // 14]
    bf16, f32 = jnp.bfloat16, jnp.float32
    anywhere = pl.BlockSpec(memory_space=pl.ANY)
    vmem = pl.BlockSpec(memory_space=pltpu.VMEM)
    dma = pltpu.SemaphoreType.DMA
    shape = jax.ShapeDtypeStruct((rows, d), bf16)
    width = qh + 2 * kh
    jobs = 2 + len(cuts)
    z_sems = dma((jobs, PLANES - 1, 3))
    out1, out2 = pl.pallas_call(
        functools.partial(kernel, n_section, (rows, d, qw, kvw)),
        out_shape=(shape, shape),
        in_specs=[anywhere] * 6 + [vmem] * 7,
        out_specs=(anywhere, anywhere),
        scratch_shapes=[
            pltpu.VMEM((d, 2 * kh), bf16),
            pltpu.VMEM((d, qh), bf16),
            *[pltpu.VMEM((qw, cut), bf16) for cut in cuts],
            pltpu.VMEM((tok, d), bf16),
            pltpu.VMEM((tok, d), bf16),
            pltpu.VMEM((tok, d), bf16),
            pltpu.VMEM((tok, width), f32),
            pltpu.VMEM((tok, HEAD_DIM), f32),
            pltpu.VMEM((2, 2, tok, HEAD_DIM), f32),
            pltpu.VMEM((2, tok, HEAD_DIM), f32),
            pltpu.VMEM((HEADS // KV_HEADS, tok, HEAD_DIM), bf16),
            *[pltpu.VMEM((HEADS // KV_HEADS, tok, HEAD_DIM), f32)] * 3,
            pltpu.VMEM((seq_len, 2 * HEAD_DIM), bf16),
            pltpu.VMEM((seq_len, 2 * HEAD_DIM), bf16),
            pltpu.VMEM((tok, seq_len), f32),
            pltpu.VMEM((tok, qw), bf16),
            pltpu.VMEM((tok, qw), bf16),
            pltpu.VMEM((tok, oh), bf16),
            pltpu.VMEM((tok, oh), bf16),
            pltpu.VMEM((tok, oh), f32),
            dma((8 + 2 * len(cuts),)),
            dma((10 + 3 * len(cuts),)),
            dma((10 + 3 * len(cuts),)),
            z_sems,
            z_sems,
            z_sems,
            z_sems,
            dma((jobs, 2 * PLANES)),
            dma((jobs, 2 * PLANES)),
            dma((2, 2, PLANES)),
            dma((2, 2, PLANES)),
            dma((len(cuts),)),
            dma((len(cuts),)),
        ],
        compiler_params=pltpu.CompilerParams(
            collective_id=0, has_side_effects=True, vmem_limit_bytes=56 * 1024 * 1024
        ),
        name="two_sections",
    )(
        activations[0],
        incoming,
        w_query[0],
        w_key[0],
        w_value[0],
        w_out[0],
        norm_gain,
        b_query,
        b_key,
        b_value,
        freqs,
        column_ids,
        positions,
    )
    return (out1[None], out2[None])


def solution(mesh):
    placed = (
        P("section", "seq", None),
        P("seq", None),
        P(),
        P(),
        P("section", None),
        P("section", "seq", None),
        P("section", "seq", None),
        P("section", "seq", None),
        P("section", "seq", None),
        P("section", None),
        P("section", None),
        P("section", None),
    )
    return jax.shard_map(
        functools.partial(per_device, mesh.shape["section"]),
        mesh=mesh,
        in_specs=placed,
        out_specs=(P("section", "seq", None), P("section", "seq", None)),
        check_vma=False,
    )
```
